32 devices in a mesh: wide: 8 (over y, x, core), narrow: 4 (over z).
Axes of the slice: x: 2, y: 2, z: 4, core: 2. Of those that a mesh axis runs over, the one named last changes fastest.
Arguments:
- state: float32 [2, 8388608], P(None, ('wide', 'narrow')), may hold values from -6 to 6
- gates: float32 [8, 2, 64, 64], replicated, may hold values from -0.5 to 0.5
- roster: int32 [10], replicated, may hold values from 0 to 7
Outputs:
- final_state: float32 [2, 8388608], P(None, ('wide', 'narrow'))
The draws below stay inside these ranges and needn't reach their ends.
All inputs are finite; a program needn't handle non-finite values.
Results may differ from the reference program's by a relative error of at most 0.00012.
Values sent between devices are 32-bit elements; how exact they have to be, the bound alone decides.
A program may use at most 64 MiB of HBM per device.

```python
import jax
import jax.numpy as jnp
from jax import lax

LOCAL = 262144
GATE = 64
BANK = 8
ROUNDS = 2
LAYERS = 10
AMPS = 8388608
N_WIDE = 8
N_NARROW = 4


def with_ends(drawn, key, least, high):
    spot = [jax.random.randint(jax.random.fold_in(key, axis), (), 0, length) for axis, length in enumerate(drawn.shape)]
    longest = drawn.shape.index(max(drawn.shape))
    neighbour = spot[:longest] + [(spot[longest] + 1) % drawn.shape[longest]] + spot[longest + 1:]
    return drawn.at[tuple(spot)].set(least).at[tuple(neighbour)].set(high)


def shard_levels(key, dims, cuts, low, largest):
    def one(dim, blocks):
        heights = jax.random.uniform(jax.random.fold_in(jax.random.fold_in(key, 6), dim), (blocks,), jnp.float32, low / len(cuts), largest / len(cuts))
        return jnp.repeat(jnp.exp(heights), dims[dim] // blocks).reshape((-1,) + (1,) * (len(dims) - dim - 1))

    factor_of = one(*cuts[0])
    for cut in cuts[1:]:
        factor_of = factor_of * one(*cut)
    return factor_of


def normal_values(rng, shape, spread, limit, shards=(), dtype=jnp.bfloat16):
    result = jax.random.normal(rng, shape, jnp.float32) * spread
    if len(shards) > 0:
        result = shard_levels(rng, shape, shards, -0.22, 0.18) * result
    return jnp.clip(result, min=-limit, max=limit).astype(dtype)


def setup_inputs(seed: int = 0) -> dict:
    arg_keys = jax.random.split(jax.random.key(seed), 4)
    state = normal_values(arg_keys[0], (2, AMPS), 1.0, 6.0, ((1, 32),), jnp.float32)
    gates = normal_values(arg_keys[1], (BANK, 2, GATE, GATE), (2 * GATE) ** -0.5, 0.5, (), jnp.float32)
    roster = with_ends(jax.random.randint(arg_keys[2], (LAYERS,), 0, BANK), jax.random.fold_in(arg_keys[2], 1), 0, BANK - 1).astype(jnp.int32)
    return dict(state=state, gates=gates, roster=roster)


def block_of(gate):
    real_part = gate[0]
    imag_part = gate[1]
    top = jnp.stack([real_part, -imag_part])
    bottom = jnp.stack([imag_part, real_part])
    return jnp.stack([top, bottom])


def apply_gate(amps, gate, low):
    view = amps.reshape(2, -1, 64, low)
    block = block_of(gate)
    out = jnp.einsum("cagb,dchg->dahb", view, block, precision=lax.Precision.HIGHEST)
    return out.reshape(2, -1)


def reference(state, gates, roster):
    top_low = LOCAL // 64
    amps = state
    for rnd in range(ROUNDS):
        k = 5 * rnd
        amps = apply_gate(amps, gates[roster[k]], 128)
        amps = apply_gate(amps, gates[roster[k + 1]], top_low)
        amps = amps.reshape(2, N_WIDE, N_NARROW, N_NARROW, LOCAL // N_NARROW).swapaxes(2, 3).reshape(2, -1)
        amps = apply_gate(amps, gates[roster[k + 2]], top_low)
        amps = amps.reshape(2, N_WIDE, N_NARROW, N_WIDE, LOCAL // N_WIDE).swapaxes(1, 3).reshape(2, -1)
        amps = apply_gate(amps, gates[roster[k + 3]], top_low)
        amps = apply_gate(amps, gates[roster[k + 4]], 128)
    return amps
```

```python
import functools

import jax
import jax.numpy as jnp
from jax import lax
from jax.experimental import pallas as pl
from jax.experimental.pallas import tpu as pltpu
from jax.sharding import PartitionSpec as P

ROUNDS = 2
GATE = 64
LANES = 128
PER_CHUNK = 4
MESH = pl.DeviceIdType.MESH


def block_of(gate):
    re, im = gate[0], gate[1]
    top = jnp.concatenate([re, -im], axis=1)
    bottom = jnp.concatenate([im, re], axis=1)
    return jnp.concatenate([top, bottom], axis=0)


def halves(value):
    high = value.astype(jnp.bfloat16)
    return high, (value - high.astype(jnp.float32)).astype(jnp.bfloat16)


def left_of(block):
    high, low = halves(block)
    top = jnp.concatenate([high, high], axis=1)
    bottom = jnp.concatenate([low, jnp.zeros_like(low)], axis=1)
    return jnp.concatenate([top, bottom], axis=0)


def apply(left, amps):
    high, low = halves(amps)
    out = jnp.dot(
        left, jnp.concatenate([high, low], axis=0), preferred_element_type=jnp.float32
    )
    return out[: 2 * GATE] + out[2 * GATE :]


def kernel(narrow, wide, gates_ref, roster_ref, x_ref, out_ref, left_ref, plane, mixed,
           send_n, recv_n, send_w, recv_w, sent_n, came_n, sent_w, came_w):
    me_n, me_w = lax.axis_index("narrow"), lax.axis_index("wide")
    blocks = x_ref.shape[0] // (2 * GATE)
    chunks = blocks // PER_CHUNK
    rows_n, rows_w = GATE // narrow, GATE // wide

    barrier = pltpu.get_barrier_semaphore()

    def greet_n(d, _):
        pl.semaphore_signal(barrier, inc=1, device_id={"narrow": lax.rem(me_n + d, narrow)}, device_id_type=MESH)
        return 0

    def greet_w(d, _):
        pl.semaphore_signal(barrier, inc=1, device_id={"wide": lax.rem(me_w + d, wide)}, device_id_type=MESH)
        return 0

    lax.fori_loop(1, narrow, greet_n, 0)
    lax.fori_loop(1, wide, greet_w, 0)

    def bank(k):
        return block_of(gates_ref[roster_ref[k]])

    left_ref[0] = left_of(bank(0))
    for rnd in range(ROUNDS):
        for i in range(1, 4):
            left_ref[4 * rnd + i] = left_of(bank(5 * rnd + i))
        last = bank(5 * rnd + 4)
        if rnd < ROUNDS - 1:
            last = jnp.dot(
                bank(5 * rnd + 5), last, precision=lax.Precision.HIGHEST,
                preferred_element_type=jnp.float32,
            )
        left_ref[4 * rnd + 4] = left_of(last)

    def first(i, _):
        x = jnp.concatenate(
            [
                jnp.concatenate(
                    [x_ref[pl.ds((2 * i + q) * 2 * GATE + c, GATE, stride=2), :] for c in range(2)],
                    axis=0,
                )
                for q in range(2)
            ],
            axis=1,
        )
        y = apply(left_ref[0], x)
        for q in range(2):
            for c in range(2):
                start = pl.multiple_of(c * blocks * GATE + (2 * i + q) * GATE, GATE)
                plane[pl.ds(start, GATE), :] = y[c * GATE:(c + 1) * GATE, q * LANES:(q + 1) * LANES]
        return 0

    lax.fori_loop(0, blocks // 2, first, 0)
    pl.semaphore_wait(barrier, narrow - 1 + wide - 1)

    for rnd in range(ROUNDS):
        def second(ch, _):
            for p in range(PER_CHUNK // 2):
                x = jnp.concatenate(
                    [
                        jnp.concatenate(
                            [
                                plane[pl.ds(c * blocks * GATE + ch * PER_CHUNK + 2 * p + q, GATE, stride=blocks), :]
                                for c in range(2)
                            ],
                            axis=0,
                        )
                        for q in range(2)
                    ],
                    axis=1,
                )
                y = apply(left_ref[4 * rnd + 1], x)
                for q in range(2):
                    for c in range(2):
                        for n in range(narrow):
                            at = ((2 * p + q) * 2 + c) * rows_n
                            send_n[rnd, ch, n, at:at + rows_n, :] = y[
                                c * GATE + n * rows_n:c * GATE + (n + 1) * rows_n,
                                q * LANES:(q + 1) * LANES,
                            ]
            for d in range(1, narrow):
                to = lax.rem(me_n + d, narrow)
                pltpu.make_async_remote_copy(
                    src_ref=send_n.at[rnd, ch, to],
                    dst_ref=recv_n.at[rnd, ch, me_n],
                    send_sem=sent_n.at[rnd, ch],
                    recv_sem=came_n.at[rnd, ch],
                    device_id={"narrow": to},
                    device_id_type=MESH,
                ).start()
            recv_n[rnd, ch, me_n] = send_n[rnd, ch, me_n]
            return 0

        def third(ch, _):
            pltpu.make_async_copy(
                send_n.at[rnd, ch, pl.ds(0, narrow - 1)],
                recv_n.at[rnd, ch, pl.ds(0, narrow - 1)],
                came_n.at[rnd, ch],
            ).wait()
            for p in range(PER_CHUNK // 2):
                x = jnp.concatenate(
                    [
                        jnp.concatenate(
                            [
                                recv_n[rnd, ch, n, pl.ds(((2 * p + q) * 2 + c) * rows_n, rows_n), :]
                                for c in range(2) for n in range(narrow)
                            ],
                            axis=0,
                        )
                        for q in range(2)
                    ],
                    axis=1,
                )
                y = apply(left_ref[4 * rnd + 2], x)
                for q in range(2):
                    for c in range(2):
                        for w in range(wide):
                            at = ((2 * p + q) * 2 + c) * rows_w
                            send_w[rnd, ch, w, at:at + rows_w, :] = y[
                                c * GATE + w * rows_w:c * GATE + (w + 1) * rows_w,
                                q * LANES:(q + 1) * LANES,
                            ]

            def push(d, _):
                to = lax.rem(me_w + d, wide)
                pltpu.make_async_remote_copy(
                    src_ref=send_w.at[rnd, ch, to],
                    dst_ref=recv_w.at[rnd, ch, me_w],
                    send_sem=sent_w.at[rnd, ch],
                    recv_sem=came_w.at[rnd, ch],
                    device_id={"wide": to},
                    device_id_type=MESH,
                ).start()
                return 0

            lax.fori_loop(1, wide, push, 0, unroll=wide <= 8)
            recv_w[rnd, ch, me_w] = send_w[rnd, ch, me_w]
            return 0

        def fourth(ch, _):
            pltpu.make_async_copy(
                send_w.at[rnd, ch, pl.ds(0, wide - 1)],
                recv_w.at[rnd, ch, pl.ds(0, wide - 1)],
                came_w.at[rnd, ch],
            ).wait()
            for p in range(PER_CHUNK // 2):
                x = jnp.concatenate(
                    [
                        jnp.concatenate(
                            [
                                recv_w[rnd, ch, w, pl.ds(((2 * p + q) * 2 + c) * rows_w, rows_w), :]
                                for c in range(2) for w in range(wide)
                            ],
                            axis=0,
                        )
                        for q in range(2)
                    ],
                    axis=1,
                )
                y = apply(left_ref[4 * rnd + 3], x)
                for q in range(2):
                    start = pl.multiple_of((ch * PER_CHUNK + 2 * p + q) * 2 * GATE, 2 * GATE)
                    mixed[pl.ds(start, 2 * GATE), :] = y[:, q * LANES:(q + 1) * LANES]
            return 0

        def fifth(i, _):
            x = jnp.concatenate(
                [
                    jnp.concatenate(
                        [
                            mixed[pl.ds(c * GATE + (2 * i + q) * 2 + b, blocks, stride=2 * GATE), :]
                            for c in range(2) for b in range(2)
                        ],
                        axis=0,
                    )
                    for q in range(2)
                ],
                axis=1,
            )
            y = apply(left_ref[4 * rnd + 4], x)
            for q in range(2):
                for c in range(2):
                    part = y[c * GATE:(c + 1) * GATE, q * LANES:(q + 1) * LANES]
                    if rnd < ROUNDS - 1:
                        start = pl.multiple_of(c * blocks * GATE + (2 * i + q) * GATE, GATE)
                        plane[pl.ds(start, GATE), :] = part
                    else:
                        out_ref[pl.ds((2 * i + q) * 2 * GATE + c, GATE, stride=2), :] = part
            return 0

        lax.fori_loop(0, chunks, second, 0)
        lax.fori_loop(0, chunks, third, 0)
        lax.fori_loop(0, chunks, fourth, 0)
        lax.fori_loop(0, blocks // 2, fifth, 0)

    def settle(ch, _):
        for rnd in range(ROUNDS):
            pltpu.make_async_copy(
                send_n.at[rnd, ch, pl.ds(0, narrow - 1)],
                recv_n.at[rnd, ch, pl.ds(0, narrow - 1)],
                sent_n.at[rnd, ch],
            ).wait()
            pltpu.make_async_copy(
                send_w.at[rnd, ch, pl.ds(0, wide - 1)],
                recv_w.at[rnd, ch, pl.ds(0, wide - 1)],
                sent_w.at[rnd, ch],
            ).wait()
        return 0

    lax.fori_loop(0, chunks, settle, 0)


def on_device(state, gates, roster):
    narrow, wide = lax.axis_size("narrow"), lax.axis_size("wide")
    rows = state.shape[1] // LANES
    blocks = rows // GATE
    chunks = blocks // PER_CHUNK
    x = state.reshape(2, rows, LANES).transpose(1, 0, 2).reshape(2 * rows, LANES)
    f32 = jnp.float32
    trade_n = pltpu.VMEM((ROUNDS, chunks, narrow, PER_CHUNK * 2 * GATE // narrow, LANES), f32)
    trade_w = pltpu.VMEM((ROUNDS, chunks, wide, PER_CHUNK * 2 * GATE // wide, LANES), f32)
    dma = pltpu.SemaphoreType.DMA((ROUNDS, chunks))
    vmem = pl.BlockSpec(memory_space=pltpu.VMEM)
    out = pl.pallas_call(
        functools.partial(kernel, narrow, wide),
        out_shape=jax.ShapeDtypeStruct((2 * rows, LANES), f32),
        in_specs=[vmem, pl.BlockSpec(memory_space=pltpu.SMEM), vmem],
        out_specs=vmem,
        scratch_shapes=[
            pltpu.VMEM((4 * ROUNDS + 1, 4 * GATE, 4 * GATE), jnp.bfloat16),
            pltpu.VMEM((2 * rows, LANES), f32),
            pltpu.VMEM((2 * rows, LANES), f32),
            trade_n, trade_n, trade_w, trade_w,
            dma, dma, dma, dma,
        ],
        compiler_params=pltpu.CompilerParams(
            collective_id=0, has_side_effects=True, vmem_limit_bytes=48 * 1024 * 1024
        ),
    )(gates, roster, x)
    return out.reshape(rows, 2, LANES).transpose(1, 0, 2).reshape(2, rows * LANES)


def solution(mesh):
    in_specs = (P(None, ("wide", "narrow")), P(), P())
    out_specs = P(None, ("wide", "narrow"))
    return jax.shard_map(
        on_device, mesh=mesh, in_specs=in_specs, out_specs=out_specs, check_vma=False
    )
```

```python
import functools

import jax
import jax.numpy as jnp
from jax import lax
from jax.experimental import pallas as pl
from jax.experimental.pallas import tpu as pltpu
from jax.sharding import PartitionSpec as P

ROUNDS = 2
GATE = 64
LANES = 128
PER_CHUNK = 4
MESH = pl.DeviceIdType.MESH


def block_of(gate):
    re, im = gate[0], gate[1]
    top = jnp.concatenate([re, -im], axis=1)
    bottom = jnp.concatenate([im, re], axis=1)
    return jnp.concatenate([top, bottom], axis=0)


def halves(value):
    high = value.astype(jnp.bfloat16)
    return high, (value - high.astype(jnp.float32)).astype(jnp.bfloat16)


def left_of(block):
    high, low = halves(block)
    top = jnp.concatenate([high, high], axis=1)
    bottom = jnp.concatenate([low, jnp.zeros_like(low)], axis=1)
    return jnp.concatenate([top, bottom], axis=0)


def apply(left, amps):
    high, low = halves(amps)
    out = jnp.dot(
        left, jnp.concatenate([high, low], axis=0), preferred_element_type=jnp.float32
    )
    return out[: 2 * GATE] + out[2 * GATE :]


def weave(first, second):
    low = lax.broadcasted_iota(jnp.int32, first.shape, 1) < LANES // 2
    turned_first = pltpu.roll(first, LANES // 2, 1)
    turned_second = pltpu.roll(second, LANES // 2, 1)
    return jnp.where(low, first, turned_second), jnp.where(low, turned_first, second)


def rows_of(parts):
    return jnp.concatenate(parts, axis=0)


def kernel(narrow, wide, gates_hbm, roster_hbm, x_hbm, out_ref, gates_ref, roster_ref, x_ref,
           left_ref, plane, mixed, send_n, recv_n, send_w, recv_w, load_sem,
           sent_n, came_n, sent_w, came_w):
    me_n, me_w = lax.axis_index("narrow"), lax.axis_index("wide")
    blocks = x_ref.shape[0] // (2 * GATE)
    half = blocks // 2
    chunks = half // PER_CHUNK
    rows_n, rows_w = GATE // narrow, GATE // wide
    split_rows = blocks * GATE
    block_rows = 2 * GATE

    loads = [
        pltpu.make_async_copy(roster_hbm, roster_ref, load_sem.at[0]),
        pltpu.make_async_copy(gates_hbm, gates_ref, load_sem.at[1]),
        pltpu.make_async_copy(x_hbm, x_ref, load_sem.at[2]),
    ]
    for load in loads:
        load.start()

    barrier = pltpu.get_barrier_semaphore()

    def greet_n(d, _):
        pl.semaphore_signal(barrier, inc=1, device_id={"narrow": lax.rem(me_n + d, narrow)}, device_id_type=MESH)
        return 0

    def greet_w(d, _):
        pl.semaphore_signal(barrier, inc=1, device_id={"wide": lax.rem(me_w + d, wide)}, device_id_type=MESH)
        return 0

    lax.fori_loop(1, narrow, greet_n, 0)
    lax.fori_loop(1, wide, greet_w, 0)

    def bank(k):
        return block_of(gates_ref[roster_ref[k]])

    loads[0].wait()
    loads[1].wait()
    for i in range(2):
        left_ref[i] = left_of(bank(i))

    def keep(split, ap, y):
        for c in range(2):
            start = pl.multiple_of(split * split_rows + c * half * GATE + ap * GATE, GATE)
            plane[pl.ds(start, GATE), :] = y[c * GATE:(c + 1) * GATE]

    def first(split):
        def step(i, _):
            parts = []
            for q in range(2):
                pair = [
                    rows_of([x_ref[pl.ds(a * block_rows + c, GATE, stride=2), :] for c in range(2)])
                    for a in (2 * i + q, 2 * i + q + half)
                ]
                parts.append(weave(*pair)[split])
            y = apply(left_ref[0], jnp.concatenate(parts, axis=1))
            for q in range(2):
                keep(split, 2 * i + q, y[:, q * LANES:(q + 1) * LANES])
            return 0

        lax.fori_loop(0, half // 2, step, 0)

    def second(phase, ch):
        rnd, split = phase // 2, phase % 2
        for p in range(PER_CHUNK // 2):
            parts = []
            for q in range(2):
                unit = ch * PER_CHUNK + 2 * p + q
                rows = []
                for c in range(2):
                    base = split * split_rows + c * half * GATE + unit
                    rows += weave(
                        plane[pl.ds(base, blocks, stride=blocks), :],
                        plane[pl.ds(base + half, blocks, stride=blocks), :],
                    )
                parts.append(rows_of(rows))
            y = apply(left_ref[4 * rnd + 1], jnp.concatenate(parts, axis=1))
            for q in range(2):
                for c in range(2):
                    for n in range(narrow):
                        at = ((2 * p + q) * 2 + c) * rows_n
                        send_n[phase, ch, n, at:at + rows_n, :] = y[
                            c * GATE + n * rows_n:c * GATE + (n + 1) * rows_n,
                            q * LANES:(q + 1) * LANES,
                        ]
        for d in range(1, narrow):
            to = lax.rem(me_n + d, narrow)
            pltpu.make_async_remote_copy(
                src_ref=send_n.at[phase, ch, to],
                dst_ref=recv_n.at[phase, ch, me_n],
                send_sem=sent_n.at[phase, ch],
                recv_sem=came_n.at[phase, ch],
                device_id={"narrow": to},
                device_id_type=MESH,
            ).start()
        recv_n[phase, ch, me_n] = send_n[phase, ch, me_n]

    def third(phase, ch):
        rnd = phase // 2
        pltpu.make_async_copy(
            send_n.at[phase, ch, pl.ds(0, narrow - 1)],
            recv_n.at[phase, ch, pl.ds(0, narrow - 1)],
            came_n.at[phase, ch],
        ).wait()
        for p in range(PER_CHUNK // 2):
            x = jnp.concatenate(
                [
                    rows_of([
                        recv_n[phase, ch, n, pl.ds(((2 * p + q) * 2 + c) * rows_n, rows_n), :]
                        for c in range(2) for n in range(narrow)
                    ])
                    for q in range(2)
                ],
                axis=1,
            )
            y = apply(left_ref[4 * rnd + 2], x)
            for q in range(2):
                for c in range(2):
                    for w in range(wide):
                        at = ((2 * p + q) * 2 + c) * rows_w
                        send_w[phase, ch, w, at:at + rows_w, :] = y[
                            c * GATE + w * rows_w:c * GATE + (w + 1) * rows_w,
                            q * LANES:(q + 1) * LANES,
                        ]

        def push(d, _):
            to = lax.rem(me_w + d, wide)
            pltpu.make_async_remote_copy(
                src_ref=send_w.at[phase, ch, to],
                dst_ref=recv_w.at[phase, ch, me_w],
                send_sem=sent_w.at[phase, ch],
                recv_sem=came_w.at[phase, ch],
                device_id={"wide": to},
                device_id_type=MESH,
            ).start()
            return 0

        lax.fori_loop(1, wide, push, 0, unroll=wide <= 8)
        recv_w[phase, ch, me_w] = send_w[phase, ch, me_w]

    def fourth(phase, ch):
        rnd, split = phase // 2, phase % 2
        pltpu.make_async_copy(
            send_w.at[phase, ch, pl.ds(0, wide - 1)],
            recv_w.at[phase, ch, pl.ds(0, wide - 1)],
            came_w.at[phase, ch],
        ).wait()
        for p in range(PER_CHUNK // 2):
            x = jnp.concatenate(
                [
                    rows_of([
                        recv_w[phase, ch, w, pl.ds(((2 * p + q) * 2 + c) * rows_w, rows_w), :]
                        for c in range(2) for w in range(wide)
                    ])
                    for q in range(2)
                ],
                axis=1,
            )
            y = apply(left_ref[4 * rnd + 3], x)
            for q in range(2):
                unit = ch * PER_CHUNK + 2 * p + q
                start = pl.multiple_of(split * split_rows + unit * block_rows, block_rows)
                mixed[pl.ds(start, block_rows), :] = y[:, q * LANES:(q + 1) * LANES]

    def fifth(phase):
        rnd, split = phase // 2, phase % 2

        def step(i, _):
            parts = []
            for q in range(2):
                pair = [
                    rows_of([
                        mixed[pl.ds(split * split_rows + c * GATE + a * 2 + b, half, stride=block_rows), :]
                        for c in range(2) for b in range(2)
                    ])
                    for a in (2 * i + q, 2 * i + q + half)
                ]
                lower, upper = weave(*pair)
                rows = []
                for k in range(4):
                    rows += [lower[k * half:(k + 1) * half], upper[k * half:(k + 1) * half]]
                parts.append(rows_of(rows))
            y = apply(left_ref[4 * rnd + 4], jnp.concatenate(parts, axis=1))
            for q in range(2):
                ap = 2 * i + q
                mine = y[:, q * LANES:(q + 1) * LANES]
                if rnd < ROUNDS - 1 or split == 0:
                    keep(split, ap, mine)
                else:
                    for c in range(2):
                        start = pl.multiple_of(c * half * GATE + ap * GATE, GATE)
                        pair = weave(plane[pl.ds(start, GATE), :], mine[c * GATE:(c + 1) * GATE])
                        for a, part in zip((ap, ap + half), pair):
                            out_ref[pl.ds(a * block_rows + c, GATE, stride=2), :] = part
            return 0

        lax.fori_loop(0, half // 2, step, 0)

    def over_chunks(body):
        def step(ch, _):
            body(ch)
            return 0

        lax.fori_loop(0, chunks, step, 0)

    loads[2].wait()
    first(0)
    pl.semaphore_wait(barrier, narrow - 1 + wide - 1)
    over_chunks(lambda ch: second(0, ch))
    first(1)
    for rnd in range(ROUNDS):
        for i in range(max(2 - 4 * rnd, 1), 4):
            if 4 * rnd + i > 1:
                left_ref[4 * rnd + i] = left_of(bank(5 * rnd + i))
        last = bank(5 * rnd + 4)
        if rnd < ROUNDS - 1:
            last = jnp.dot(
                bank(5 * rnd + 5), last, precision=lax.Precision.HIGHEST,
                preferred_element_type=jnp.float32,
            )
        left_ref[4 * rnd + 4] = left_of(last)

    for phase in range(2 * ROUNDS):
        def exchange(ch, phase=phase):
            third(phase, ch)
            if phase + 1 < 2 * ROUNDS:
                second(phase + 1, ch)

        over_chunks(exchange)
        over_chunks(functools.partial(fourth, phase))
        fifth(phase)

    def settle(ch):
        for phase in range(2 * ROUNDS):
            pltpu.make_async_copy(
                send_n.at[phase, ch, pl.ds(0, narrow - 1)],
                recv_n.at[phase, ch, pl.ds(0, narrow - 1)],
                sent_n.at[phase, ch],
            ).wait()
            pltpu.make_async_copy(
                send_w.at[phase, ch, pl.ds(0, wide - 1)],
                recv_w.at[phase, ch, pl.ds(0, wide - 1)],
                sent_w.at[phase, ch],
            ).wait()

    over_chunks(settle)


def on_device(state, gates, roster):
    narrow, wide = lax.axis_size("narrow"), lax.axis_size("wide")
    rows = state.shape[1] // LANES
    chunks = rows // GATE // 2 // PER_CHUNK
    phases = 2 * ROUNDS
    x = state.reshape(2, rows, LANES).transpose(1, 0, 2).reshape(2 * rows, LANES)
    f32 = jnp.float32
    trade_n = pltpu.VMEM((phases, chunks, narrow, PER_CHUNK * 2 * GATE // narrow, LANES), f32)
    trade_w = pltpu.VMEM((phases, chunks, wide, PER_CHUNK * 2 * GATE // wide, LANES), f32)
    dma = pltpu.SemaphoreType.DMA((phases, chunks))
    hbm = pl.BlockSpec(memory_space=pltpu.HBM)
    whole = pltpu.VMEM((2 * rows, LANES), f32)
    out = pl.pallas_call(
        functools.partial(kernel, narrow, wide),
        out_shape=jax.ShapeDtypeStruct((2 * rows, LANES), f32),
        in_specs=[hbm, hbm, hbm],
        out_specs=pl.BlockSpec(memory_space=pltpu.VMEM),
        scratch_shapes=[
            pltpu.VMEM(gates.shape, f32),
            pltpu.SMEM(roster.shape, jnp.int32),
            whole,
            pltpu.VMEM((4 * ROUNDS + 1, 4 * GATE, 4 * GATE), jnp.bfloat16),
            whole, whole,
            trade_n, trade_n, trade_w, trade_w,
            pltpu.SemaphoreType.DMA((3,)),
            dma, dma, dma, dma,
        ],
        compiler_params=pltpu.CompilerParams(
            collective_id=0, has_side_effects=True, vmem_limit_bytes=64 * 1024 * 1024
        ),
    )(gates, roster, x)
    return out.reshape(rows, 2, LANES).transpose(1, 0, 2).reshape(2, rows * LANES)


def solution(mesh):
    in_specs = (P(None, ("wide", "narrow")), P(), P())
    out_specs = P(None, ("wide", "narrow"))
    return jax.shard_map(
        on_device, mesh=mesh, in_specs=in_specs, out_specs=out_specs, check_vma=False
    )
```

```python
import functools

import jax
import jax.numpy as jnp
from jax import lax
from jax.experimental import pallas as pl
from jax.experimental.pallas import tpu as pltpu
from jax.sharding import PartitionSpec as P

ROUNDS = 2
GATE = 64
LANES = 128
PER_CHUNK = 2
MESH = pl.DeviceIdType.MESH


def block_of(gate):
    re, im = gate[0], gate[1]
    top = jnp.concatenate([re, -im], axis=1)
    bottom = jnp.concatenate([im, re], axis=1)
    return jnp.concatenate([top, bottom], axis=0)


def halves(value):
    high = value.astype(jnp.bfloat16)
    return high, (value - high.astype(jnp.float32)).astype(jnp.bfloat16)


def left_of(block):
    high, low = halves(block)
    top = jnp.concatenate([high, high], axis=1)
    bottom = jnp.concatenate([low, jnp.zeros_like(low)], axis=1)
    return jnp.concatenate([top, bottom], axis=0)


def apply(left, amps):
    high, low = halves(amps)
    out = jnp.dot(
        left, jnp.concatenate([high, low], axis=0), preferred_element_type=jnp.float32
    )
    return out[: 2 * GATE] + out[2 * GATE :]


def weave(first, second):
    low = lax.broadcasted_iota(jnp.int32, first.shape, 1) < LANES // 2
    turned_first = pltpu.roll(first, LANES // 2, 1)
    turned_second = pltpu.roll(second, LANES // 2, 1)
    return jnp.where(low, first, turned_second), jnp.where(low, turned_first, second)


def rows_of(parts):
    return jnp.concatenate(parts, axis=0)


def farthest_first(count):
    return [d for d in range(count // 2, count)] + [d for d in range(1, count // 2)]


def partner(me, distance, count):
    to, bit = 0, 1
    while bit < count:
        mine = lax.rem(lax.div(me, bit), 2)
        to = to + bit * (1 - mine if distance & bit else mine)
        bit *= 2
    return to


def kernel(narrow, wide, gates_hbm, roster_hbm, x_hbm, out_ref, gates_ref, roster_ref, x_ref,
           left_ref, plane, mixed, send_n, recv_n, send_w, recv_w, load_sem,
           sent_n, came_n, sent_w, came_w):
    me_n, me_w = lax.axis_index("narrow"), lax.axis_index("wide")
    blocks = x_ref.shape[0] // (2 * GATE)
    half = blocks // 2
    chunks = half // PER_CHUNK
    rows_n, rows_w = GATE // narrow, GATE // wide
    split_rows = blocks * GATE
    block_rows = 2 * GATE

    loads = [
        pltpu.make_async_copy(roster_hbm, roster_ref, load_sem.at[0]),
        pltpu.make_async_copy(gates_hbm, gates_ref, load_sem.at[1]),
        pltpu.make_async_copy(x_hbm, x_ref, load_sem.at[2]),
    ]
    for load in loads:
        load.start()

    barrier = pltpu.get_barrier_semaphore()

    def greet_n(d, _):
        pl.semaphore_signal(barrier, inc=1, device_id={"narrow": lax.rem(me_n + d, narrow)}, device_id_type=MESH)
        return 0

    def greet_w(d, _):
        pl.semaphore_signal(barrier, inc=1, device_id={"wide": lax.rem(me_w + d, wide)}, device_id_type=MESH)
        return 0

    lax.fori_loop(1, narrow, greet_n, 0)
    lax.fori_loop(1, wide, greet_w, 0)

    def bank(k):
        return block_of(gates_ref[roster_ref[k]])

    loads[0].wait()
    loads[1].wait()
    for i in range(2):
        left_ref[i] = left_of(bank(i))

    def keep(split, ap, y):
        for c in range(2):
            start = pl.multiple_of(split * split_rows + c * half * GATE + ap * GATE, GATE)
            plane[pl.ds(start, GATE), :] = y[c * GATE:(c + 1) * GATE]

    def first(split):
        def step(i, _):
            parts = []
            for q in range(2):
                pair = [
                    rows_of([x_ref[pl.ds(a * block_rows + c, GATE, stride=2), :] for c in range(2)])
                    for a in (2 * i + q, 2 * i + q + half)
                ]
                parts.append(weave(*pair)[split])
            y = apply(left_ref[0], jnp.concatenate(parts, axis=1))
            for q in range(2):
                keep(split, 2 * i + q, y[:, q * LANES:(q + 1) * LANES])
            return 0

        lax.fori_loop(0, half // 2, step, 0)

    def second(phase, ch):
        rnd, split = phase // 2, phase % 2
        for p in range(PER_CHUNK // 2):
            parts = []
            for q in range(2):
                unit = ch * PER_CHUNK + 2 * p + q
                rows = []
                for c in range(2):
                    base = split * split_rows + c * half * GATE + unit
                    rows += weave(
                        plane[pl.ds(base, blocks, stride=blocks), :],
                        plane[pl.ds(base + half, blocks, stride=blocks), :],
                    )
                parts.append(rows_of(rows))
            y = apply(left_ref[4 * rnd + 1], jnp.concatenate(parts, axis=1))
            for q in range(2):
                for c in range(2):
                    for n in range(narrow):
                        at = ((2 * p + q) * 2 + c) * rows_n
                        send_n[phase, ch, n, at:at + rows_n, :] = y[
                            c * GATE + n * rows_n:c * GATE + (n + 1) * rows_n,
                            q * LANES:(q + 1) * LANES,
                        ]
        for d in farthest_first(narrow):
            to = partner(me_n, d, narrow)
            pltpu.make_async_remote_copy(
                src_ref=send_n.at[phase, ch, to],
                dst_ref=recv_n.at[phase, ch, me_n],
                send_sem=sent_n.at[phase, ch],
                recv_sem=came_n.at[phase, ch],
                device_id={"narrow": to},
                device_id_type=MESH,
            ).start()
        recv_n[phase, ch, me_n] = send_n[phase, ch, me_n]

    def third(phase, ch):
        rnd = phase // 2
        pltpu.make_async_copy(
            send_n.at[phase, ch, pl.ds(0, narrow - 1)],
            recv_n.at[phase, ch, pl.ds(0, narrow - 1)],
            came_n.at[phase, ch],
        ).wait()
        for p in range(PER_CHUNK // 2):
            x = jnp.concatenate(
                [
                    rows_of([
                        recv_n[phase, ch, n, pl.ds(((2 * p + q) * 2 + c) * rows_n, rows_n), :]
                        for c in range(2) for n in range(narrow)
                    ])
                    for q in range(2)
                ],
                axis=1,
            )
            y = apply(left_ref[4 * rnd + 2], x)
            for q in range(2):
                for c in range(2):
                    for w in range(wide):
                        at = ((2 * p + q) * 2 + c) * rows_w
                        send_w[phase, ch, w, at:at + rows_w, :] = y[
                            c * GATE + w * rows_w:c * GATE + (w + 1) * rows_w,
                            q * LANES:(q + 1) * LANES,
                        ]

        def push(d, _):
            to = lax.rem(me_w + d, wide)
            pltpu.make_async_remote_copy(
                src_ref=send_w.at[phase, ch, to],
                dst_ref=recv_w.at[phase, ch, me_w],
                send_sem=sent_w.at[phase, ch],
                recv_sem=came_w.at[phase, ch],
                device_id={"wide": to},
                device_id_type=MESH,
            ).start()
            return 0

        lax.fori_loop(1, wide, push, 0, unroll=wide <= 8)
        recv_w[phase, ch, me_w] = send_w[phase, ch, me_w]

    def fourth(phase, ch):
        rnd, split = phase // 2, phase % 2
        pltpu.make_async_copy(
            send_w.at[phase, ch, pl.ds(0, wide - 1)],
            recv_w.at[phase, ch, pl.ds(0, wide - 1)],
            came_w.at[phase, ch],
        ).wait()
        for p in range(PER_CHUNK // 2):
            x = jnp.concatenate(
                [
                    rows_of([
                        recv_w[phase, ch, w, pl.ds(((2 * p + q) * 2 + c) * rows_w, rows_w), :]
                        for c in range(2) for w in range(wide)
                    ])
                    for q in range(2)
                ],
                axis=1,
            )
            y = apply(left_ref[4 * rnd + 3], x)
            for q in range(2):
                unit = ch * PER_CHUNK + 2 * p + q
                start = pl.multiple_of(split * split_rows + unit * block_rows, block_rows)
                mixed[pl.ds(start, block_rows), :] = y[:, q * LANES:(q + 1) * LANES]

    def fifth(phase):
        rnd, split = phase // 2, phase % 2

        def step(i, _):
            parts = []
            for q in range(2):
                pair = [
                    rows_of([
                        mixed[pl.ds(split * split_rows + c * GATE + a * 2 + b, half, stride=block_rows), :]
                        for c in range(2) for b in range(2)
                    ])
                    for a in (2 * i + q, 2 * i + q + half)
                ]
                lower, upper = weave(*pair)
                rows = []
                for k in range(4):
                    rows += [lower[k * half:(k + 1) * half], upper[k * half:(k + 1) * half]]
                parts.append(rows_of(rows))
            y = apply(left_ref[4 * rnd + 4], jnp.concatenate(parts, axis=1))
            for q in range(2):
                ap = 2 * i + q
                mine = y[:, q * LANES:(q + 1) * LANES]
                if rnd < ROUNDS - 1 or split == 0:
                    keep(split, ap, mine)
                else:
                    for c in range(2):
                        start = pl.multiple_of(c * half * GATE + ap * GATE, GATE)
                        pair = weave(plane[pl.ds(start, GATE), :], mine[c * GATE:(c + 1) * GATE])
                        for a, part in zip((ap, ap + half), pair):
                            out_ref[pl.ds(a * block_rows + c, GATE, stride=2), :] = part
            return 0

        lax.fori_loop(0, half // 2, step, 0)

    def over_chunks(body, begin=0, end=chunks):
        def step(ch, _):
            body(ch)
            return 0

        lax.fori_loop(begin, end, step, 0)

    loads[2].wait()
    first(0)
    pl.semaphore_wait(barrier, narrow - 1 + wide - 1)
    over_chunks(lambda ch: second(0, ch))
    first(1)
    for rnd in range(ROUNDS):
        for i in range(max(2 - 4 * rnd, 1), 4):
            if 4 * rnd + i > 1:
                left_ref[4 * rnd + i] = left_of(bank(5 * rnd + i))
        last = bank(5 * rnd + 4)
        if rnd < ROUNDS - 1:
            last = jnp.dot(
                bank(5 * rnd + 5), last, precision=lax.Precision.HIGHEST,
                preferred_element_type=jnp.float32,
            )
        left_ref[4 * rnd + 4] = left_of(last)

    for phase in range(2 * ROUNDS):
        def exchange(ch, phase=phase):
            third(phase, ch)
            if phase + 1 < 2 * ROUNDS:
                second(phase + 1, ch)

        if phase + 1 < 2 * ROUNDS:
            over_chunks(exchange)
            over_chunks(functools.partial(fourth, phase))
        else:
            def drain(ch, phase=phase):
                third(phase, ch)
                fourth(phase, ch - 2)

            over_chunks(exchange, 0, 2)
            over_chunks(drain, 2, chunks)
            over_chunks(functools.partial(fourth, phase), chunks - 2, chunks)
        fifth(phase)

    def settle(ch):
        for phase in range(2 * ROUNDS):
            pltpu.make_async_copy(
                send_n.at[phase, ch, pl.ds(0, narrow - 1)],
                recv_n.at[phase, ch, pl.ds(0, narrow - 1)],
                sent_n.at[phase, ch],
            ).wait()
            pltpu.make_async_copy(
                send_w.at[phase, ch, pl.ds(0, wide - 1)],
                recv_w.at[phase, ch, pl.ds(0, wide - 1)],
                sent_w.at[phase, ch],
            ).wait()

    over_chunks(settle)


def on_device(state, gates, roster):
    narrow, wide = lax.axis_size("narrow"), lax.axis_size("wide")
    rows = state.shape[1] // LANES
    chunks = rows // GATE // 2 // PER_CHUNK
    phases = 2 * ROUNDS
    x = state.reshape(2, rows, LANES).transpose(1, 0, 2).reshape(2 * rows, LANES)
    f32 = jnp.float32
    trade_n = pltpu.VMEM((phases, chunks, narrow, PER_CHUNK * 2 * GATE // narrow, LANES), f32)
    trade_w = pltpu.VMEM((phases, chunks, wide, PER_CHUNK * 2 * GATE // wide, LANES), f32)
    dma = pltpu.SemaphoreType.DMA((phases, chunks))
    hbm = pl.BlockSpec(memory_space=pltpu.HBM)
    whole = pltpu.VMEM((2 * rows, LANES), f32)
    out = pl.pallas_call(
        functools.partial(kernel, narrow, wide),
        out_shape=jax.ShapeDtypeStruct((2 * rows, LANES), f32),
        in_specs=[hbm, hbm, hbm],
        out_specs=pl.BlockSpec(memory_space=pltpu.VMEM),
        scratch_shapes=[
            pltpu.VMEM(gates.shape, f32),
            pltpu.SMEM(roster.shape, jnp.int32),
            whole,
            pltpu.VMEM((4 * ROUNDS + 1, 4 * GATE, 4 * GATE), jnp.bfloat16),
            whole, whole,
            trade_n, trade_n, trade_w, trade_w,
            pltpu.SemaphoreType.DMA((3,)),
            dma, dma, dma, dma,
        ],
        compiler_params=pltpu.CompilerParams(
            collective_id=0, has_side_effects=True, vmem_limit_bytes=64 * 1024 * 1024
        ),
    )(gates, roster, x)
    return out.reshape(rows, 2, LANES).transpose(1, 0, 2).reshape(2, rows * LANES)


def solution(mesh):
    in_specs = (P(None, ("wide", "narrow")), P(), P())
    out_specs = P(None, ("wide", "narrow"))
    return jax.shard_map(
        on_device, mesh=mesh, in_specs=in_specs, out_specs=out_specs, check_vma=False
    )
```

```python
import functools

import jax
import jax.numpy as jnp
from jax import lax
from jax.experimental import pallas as pl
from jax.experimental.pallas import tpu as pltpu
from jax.sharding import PartitionSpec as P

ROUNDS = 2
GATE = 64
LANES = 128
PER_CHUNK = 4
PIECES = 4
MESH = pl.DeviceIdType.MESH


def block_of(gate):
    re, im = gate[0], gate[1]
    top = jnp.concatenate([re, -im], axis=1)
    bottom = jnp.concatenate([im, re], axis=1)
    return jnp.concatenate([top, bottom], axis=0)


def halves(value):
    high = value.astype(jnp.bfloat16)
    return high, (value - high.astype(jnp.float32)).astype(jnp.bfloat16)


def left_of(block):
    high, low = halves(block)
    top = jnp.concatenate([high, high], axis=1)
    bottom = jnp.concatenate([low, jnp.zeros_like(low)], axis=1)
    return jnp.concatenate([top, bottom], axis=0)


def apply(left, amps):
    high, low = halves(amps)
    out = jnp.dot(
        left, jnp.concatenate([high, low], axis=0), preferred_element_type=jnp.float32
    )
    return out[: 2 * GATE] + out[2 * GATE :]


def weave(first, second):
    low = lax.broadcasted_iota(jnp.int32, first.shape, 1) < LANES // 2
    turned_first = pltpu.roll(first, LANES // 2, 1)
    turned_second = pltpu.roll(second, LANES // 2, 1)
    return jnp.where(low, first, turned_second), jnp.where(low, turned_first, second)


def rows_of(parts):
    return jnp.concatenate(parts, axis=0)


def in_order(first, second):
    lower, upper = weave(first, second)
    half = first.shape[0] // 4
    rows = []
    for k in range(4):
        rows += [lower[k * half:(k + 1) * half], upper[k * half:(k + 1) * half]]
    return rows_of(rows)


def closing(left_ref, kept_ref, mixed_ref, out_ref):
    units, pairs = mixed_ref.shape[0], kept_ref.shape[1] // GATE
    flat = mixed_ref.reshape(units * 4 * 2 * pairs, LANES)
    left = left_ref[...]
    for p in range(pairs // 2):
        parts = []
        for q in range(2):
            ap = 2 * p + q
            pair = [
                rows_of([
                    flat[pl.ds((c * 2 + h) * 2 * pairs + ap * 2 + b, units, stride=8 * pairs), :]
                    for c in range(2) for b in range(2)
                ])
                for h in range(2)
            ]
            parts.append(in_order(*pair))
        y = apply(left, jnp.concatenate(parts, axis=1))
        for q in range(2):
            ap = 2 * p + q
            for c in range(2):
                pair = weave(
                    kept_ref[c, ap * GATE:(ap + 1) * GATE, :],
                    y[c * GATE:(c + 1) * GATE, q * LANES:(q + 1) * LANES],
                )
                for h in range(2):
                    out_ref[h, pl.ds(ap * 2 * GATE + c, GATE, stride=2), :] = pair[h]


def kernel(narrow, wide, gates_hbm, roster_hbm, x_hbm, kept_hbm, mixed_hbm, last_hbm,
           gates_ref, roster_ref, x_ref, left_ref, plane, mixed, send_n, recv_n, send_w, recv_w,
           load_sem, x_sem, kept_sem, last_sem, mixed_sem, sent_n, came_n, sent_w, came_w):
    me_n, me_w = lax.axis_index("narrow"), lax.axis_index("wide")
    blocks = x_ref.shape[0] // (2 * GATE)
    half = blocks // 2
    chunks = half // PER_CHUNK
    rows_n, rows_w = GATE // narrow, GATE // wide
    split_rows = blocks * GATE
    block_rows = 2 * GATE

    loads = [
        pltpu.make_async_copy(roster_hbm, roster_ref, load_sem.at[0]),
        pltpu.make_async_copy(gates_hbm, gates_ref, load_sem.at[1]),
    ]
    for load in loads:
        load.start()
    piece = half // PIECES

    def x_load(p, h):
        rows = pl.ds(pl.multiple_of((h * half + p * piece) * block_rows, block_rows), piece * block_rows)
        return pltpu.make_async_copy(x_hbm.at[rows], x_ref.at[rows], x_sem.at[p, h])

    for p in range(PIECES):
        for h in range(2):
            x_load(p, h).start()

    barrier = pltpu.get_barrier_semaphore()

    def greet_n(d, _):
        pl.semaphore_signal(barrier, inc=1, device_id={"narrow": lax.rem(me_n + d, narrow)}, device_id_type=MESH)
        return 0

    def greet_w(d, _):
        pl.semaphore_signal(barrier, inc=1, device_id={"wide": lax.rem(me_w + d, wide)}, device_id_type=MESH)
        return 0

    lax.fori_loop(1, narrow, greet_n, 0)
    lax.fori_loop(1, wide, greet_w, 0)

    def bank(k):
        return block_of(gates_ref[roster_ref[k]])

    loads[0].wait()
    loads[1].wait()
    for i in range(2):
        left_ref[i] = left_of(bank(i))

    def keep(split, ap, y):
        for c in range(2):
            start = pl.multiple_of(split * split_rows + c * half * GATE + ap * GATE, GATE)
            plane[pl.ds(start, GATE), :] = y[c * GATE:(c + 1) * GATE]

    def first(split):
        def step(i, _):
            parts = []
            for q in range(2):
                pair = [
                    rows_of([x_ref[pl.ds(a * block_rows + c, GATE, stride=2), :] for c in range(2)])
                    for a in (2 * i + q, 2 * i + q + half)
                ]
                parts.append(weave(*pair)[split])
            y = apply(left_ref[0], jnp.concatenate(parts, axis=1))
            for q in range(2):
                keep(split, 2 * i + q, y[:, q * LANES:(q + 1) * LANES])
            return 0

        def steps(p, _):
            if split == 0:
                for h in range(2):
                    x_load(p, h).wait()
            lax.fori_loop(p * (piece // 2), (p + 1) * (piece // 2), step, 0)
            return 0

        lax.fori_loop(0, PIECES, steps, 0)

    def second(phase, ch):
        rnd, split = phase // 2, phase % 2
        for p in range(PER_CHUNK // 2):
            parts = []
            for q in range(2):
                unit = ch * PER_CHUNK + 2 * p + q
                rows = []
                for c in range(2):
                    base = split * split_rows + c * half * GATE + unit
                    rows += weave(
                        plane[pl.ds(base, blocks, stride=blocks), :],
                        plane[pl.ds(base + half, blocks, stride=blocks), :],
                    )
                parts.append(rows_of(rows))
            y = apply(left_ref[4 * rnd + 1], jnp.concatenate(parts, axis=1))
            for q in range(2):
                for c in range(2):
                    for n in range(narrow):
                        at = ((2 * p + q) * 2 + c) * rows_n
                        send_n[phase, ch, n, at:at + rows_n, :] = y[
                            c * GATE + n * rows_n:c * GATE + (n + 1) * rows_n,
                            q * LANES:(q + 1) * LANES,
                        ]
        for d in range(1, narrow):
            to = lax.rem(me_n + d, narrow)
            pltpu.make_async_remote_copy(
                src_ref=send_n.at[phase, ch, to],
                dst_ref=recv_n.at[phase, ch, me_n],
                send_sem=sent_n.at[phase, ch],
                recv_sem=came_n.at[phase, ch],
                device_id={"narrow": to},
                device_id_type=MESH,
            ).start()
        recv_n[phase, ch, me_n] = send_n[phase, ch, me_n]

    def third(phase, ch):
        rnd = phase // 2
        pltpu.make_async_copy(
            send_n.at[phase, ch, pl.ds(0, narrow - 1)],
            recv_n.at[phase, ch, pl.ds(0, narrow - 1)],
            came_n.at[phase, ch],
        ).wait()
        for p in range(PER_CHUNK // 2):
            x = jnp.concatenate(
                [
                    rows_of([
                        recv_n[phase, ch, n, pl.ds(((2 * p + q) * 2 + c) * rows_n, rows_n), :]
                        for c in range(2) for n in range(narrow)
                    ])
                    for q in range(2)
                ],
                axis=1,
            )
            y = apply(left_ref[4 * rnd + 2], x)
            for q in range(2):
                for c in range(2):
                    for w in range(wide):
                        at = ((2 * p + q) * 2 + c) * rows_w
                        send_w[phase, ch, w, at:at + rows_w, :] = y[
                            c * GATE + w * rows_w:c * GATE + (w + 1) * rows_w,
                            q * LANES:(q + 1) * LANES,
                        ]

        def push(d, _):
            to = lax.rem(me_w + d, wide)
            pltpu.make_async_remote_copy(
                src_ref=send_w.at[phase, ch, to],
                dst_ref=recv_w.at[phase, ch, me_w],
                send_sem=sent_w.at[phase, ch],
                recv_sem=came_w.at[phase, ch],
                device_id={"wide": to},
                device_id_type=MESH,
            ).start()
            return 0

        lax.fori_loop(1, wide, push, 0, unroll=wide <= 8)
        recv_w[phase, ch, me_w] = send_w[phase, ch, me_w]

    def fourth(phase, ch):
        rnd, split = phase // 2, phase % 2
        pltpu.make_async_copy(
            send_w.at[phase, ch, pl.ds(0, wide - 1)],
            recv_w.at[phase, ch, pl.ds(0, wide - 1)],
            came_w.at[phase, ch],
        ).wait()
        for p in range(PER_CHUNK // 2):
            x = jnp.concatenate(
                [
                    rows_of([
                        recv_w[phase, ch, w, pl.ds(((2 * p + q) * 2 + c) * rows_w, rows_w), :]
                        for c in range(2) for w in range(wide)
                    ])
                    for q in range(2)
                ],
                axis=1,
            )
            y = apply(left_ref[4 * rnd + 3], x)
            for q in range(2):
                unit = ch * PER_CHUNK + 2 * p + q
                start = pl.multiple_of(split * split_rows + unit * block_rows, block_rows)
                mixed[pl.ds(start, block_rows), :] = y[:, q * LANES:(q + 1) * LANES]

    def fifth(phase):
        rnd, split = phase // 2, phase % 2

        def step(i, _):
            parts = []
            for q in range(2):
                pair = [
                    rows_of([
                        mixed[pl.ds(split * split_rows + c * GATE + a * 2 + b, half, stride=block_rows), :]
                        for c in range(2) for b in range(2)
                    ])
                    for a in (2 * i + q, 2 * i + q + half)
                ]
                parts.append(in_order(*pair))
            y = apply(left_ref[4 * rnd + 4], jnp.concatenate(parts, axis=1))
            for q in range(2):
                ap = 2 * i + q
                keep(split, ap, y[:, q * LANES:(q + 1) * LANES])
            return 0

        lax.fori_loop(0, half // 2, step, 0)

    def over_chunks(body):
        def step(ch, _):
            body(ch)
            return 0

        lax.fori_loop(0, chunks, step, 0)

    first(0)
    pl.semaphore_wait(barrier, narrow - 1 + wide - 1)
    over_chunks(lambda ch: second(0, ch))
    first(1)
    for rnd in range(ROUNDS):
        for i in range(max(2 - 4 * rnd, 1), 4):
            if 4 * rnd + i > 1:
                left_ref[4 * rnd + i] = left_of(bank(5 * rnd + i))
        last = bank(5 * rnd + 4)
        if rnd < ROUNDS - 1:
            last = jnp.dot(
                bank(5 * rnd + 5), last, precision=lax.Precision.HIGHEST,
                preferred_element_type=jnp.float32,
            )
        left_ref[4 * rnd + 4] = left_of(last)

    last_out = pltpu.make_async_copy(left_ref.at[4 * ROUNDS], last_hbm, last_sem)
    last_out.start()
    kept_out = pltpu.make_async_copy(plane.at[pl.ds(0, split_rows)], kept_hbm, kept_sem)

    def mixed_out(ch):
        rows = PER_CHUNK * block_rows
        start = pl.multiple_of(ch * rows, rows)
        return pltpu.make_async_copy(
            mixed.at[pl.ds(split_rows + start, rows)], mixed_hbm.at[pl.ds(start, rows)], mixed_sem.at[ch]
        )

    def ending(ch):
        fourth(2 * ROUNDS - 1, ch)
        mixed_out(ch).start()

    for phase in range(2 * ROUNDS):
        def exchange(ch, phase=phase):
            third(phase, ch)
            if phase + 1 < 2 * ROUNDS:
                second(phase + 1, ch)

        over_chunks(exchange)
        if phase + 1 < 2 * ROUNDS:
            over_chunks(functools.partial(fourth, phase))
            fifth(phase)
            if phase == 2 * ROUNDS - 2:
                kept_out.start()
        else:
            over_chunks(ending)

    def settle(ch):
        for phase in range(2 * ROUNDS):
            pltpu.make_async_copy(
                send_n.at[phase, ch, pl.ds(0, narrow - 1)],
                recv_n.at[phase, ch, pl.ds(0, narrow - 1)],
                sent_n.at[phase, ch],
            ).wait()
            pltpu.make_async_copy(
                send_w.at[phase, ch, pl.ds(0, wide - 1)],
                recv_w.at[phase, ch, pl.ds(0, wide - 1)],
                sent_w.at[phase, ch],
            ).wait()

    over_chunks(settle)
    last_out.wait()
    kept_out.wait()
    over_chunks(lambda ch: mixed_out(ch).wait())


def on_device(state, gates, roster):
    narrow, wide = lax.axis_size("narrow"), lax.axis_size("wide")
    rows = state.shape[1] // LANES
    chunks = rows // GATE // 2 // PER_CHUNK
    phases = 2 * ROUNDS
    x = state.reshape(2, rows, LANES).transpose(1, 0, 2).reshape(2 * rows, LANES)
    f32 = jnp.float32
    trade_n = pltpu.VMEM((phases, chunks, narrow, PER_CHUNK * 2 * GATE // narrow, LANES), f32)
    trade_w = pltpu.VMEM((phases, chunks, wide, PER_CHUNK * 2 * GATE // wide, LANES), f32)
    dma = pltpu.SemaphoreType.DMA((phases, chunks))
    hbm = pl.BlockSpec(memory_space=pltpu.HBM)
    whole = pltpu.VMEM((2 * rows, LANES), f32)
    half_state = jax.ShapeDtypeStruct((rows, LANES), f32)
    factor = jax.ShapeDtypeStruct((4 * GATE, 4 * GATE), jnp.bfloat16)
    kept, mixed, last = pl.pallas_call(
        functools.partial(kernel, narrow, wide),
        out_shape=[half_state, half_state, factor],
        in_specs=[hbm, hbm, hbm],
        out_specs=[hbm, hbm, hbm],
        scratch_shapes=[
            pltpu.VMEM(gates.shape, f32),
            pltpu.SMEM(roster.shape, jnp.int32),
            whole,
            pltpu.VMEM((4 * ROUNDS + 1, 4 * GATE, 4 * GATE), jnp.bfloat16),
            whole, whole,
            trade_n, trade_n, trade_w, trade_w,
            pltpu.SemaphoreType.DMA((2,)),
            pltpu.SemaphoreType.DMA((PIECES, 2)),
            pltpu.SemaphoreType.DMA, pltpu.SemaphoreType.DMA,
            pltpu.SemaphoreType.DMA((chunks,)),
            dma, dma, dma, dma,
        ],
        compiler_params=pltpu.CompilerParams(
            collective_id=0, has_side_effects=True, vmem_limit_bytes=64 * 1024 * 1024
        ),
    )(gates, roster, x)

    half = rows // GATE // 2
    pairs = half // PIECES
    out = pl.pallas_call(
        closing,
        grid=(PIECES,),
        out_shape=jax.ShapeDtypeStruct((2, rows, LANES), f32),
        in_specs=[
            pl.BlockSpec((4 * GATE, 4 * GATE), lambda i: (0, 0)),
            pl.BlockSpec((2, pairs * GATE, LANES), lambda i: (0, i, 0)),
            pl.BlockSpec((half, 2, 2, 2 * pairs, LANES), lambda i: (0, 0, 0, i, 0)),
        ],
        out_specs=pl.BlockSpec((2, pairs * 2 * GATE, LANES), lambda i: (0, i, 0)),
        compiler_params=pltpu.CompilerParams(vmem_limit_bytes=64 * 1024 * 1024),
    )(last, kept.reshape(2, half * GATE, LANES), mixed.reshape(half, 2, 2, GATE // 2, LANES))
    return out.reshape(rows, 2, LANES).transpose(1, 0, 2).reshape(2, rows * LANES)


def solution(mesh):
    in_specs = (P(None, ("wide", "narrow")), P(), P())
    out_specs = P(None, ("wide", "narrow"))
    return jax.shard_map(
        on_device, mesh=mesh, in_specs=in_specs, out_specs=out_specs, check_vma=False
    )
```

```python
import functools

import jax
import jax.numpy as jnp
from jax import lax
from jax.experimental import pallas as pl
from jax.experimental.pallas import tpu as pltpu
from jax.sharding import PartitionSpec as P

ROUNDS = 2
GATE = 64
LANES = 128
PER_CHUNK = 4
PIECES = 4
AT_ONCE = 4
MESH = pl.DeviceIdType.MESH


def block_of(gate):
    re, im = gate[0], gate[1]
    top = jnp.concatenate([re, -im], axis=1)
    bottom = jnp.concatenate([im, re], axis=1)
    return jnp.concatenate([top, bottom], axis=0)


def halves(value):
    high = value.astype(jnp.bfloat16)
    return high, (value - high.astype(jnp.float32)).astype(jnp.bfloat16)


def left_of(block):
    high, low = halves(block)
    top = jnp.concatenate([high, high], axis=1)
    bottom = jnp.concatenate([low, jnp.zeros_like(low)], axis=1)
    return jnp.concatenate([top, bottom], axis=0)


def apply(left, amps):
    high, low = halves(amps)
    out = jnp.dot(
        left, jnp.concatenate([high, low], axis=0), preferred_element_type=jnp.float32
    )
    return out[: 2 * GATE] + out[2 * GATE :]


def weave(first, second):
    low = lax.broadcasted_iota(jnp.int32, first.shape, 1) < LANES // 2
    turned_first = pltpu.roll(first, LANES // 2, 1)
    turned_second = pltpu.roll(second, LANES // 2, 1)
    return jnp.where(low, first, turned_second), jnp.where(low, turned_first, second)


def rows_of(parts):
    return jnp.concatenate(parts, axis=0)


def in_order(first, second):
    lower, upper = weave(first, second)
    half = first.shape[0] // 4
    rows = []
    for k in range(4):
        rows += [lower[k * half:(k + 1) * half], upper[k * half:(k + 1) * half]]
    return rows_of(rows)


def closing(left_ref, kept_ref, mixed_ref, out_ref):
    units, pairs = mixed_ref.shape[0], kept_ref.shape[1] // GATE
    flat = mixed_ref.reshape(units * 4 * 2 * pairs, LANES)
    left = left_ref[...]
    for p in range(pairs // AT_ONCE):
        parts = []
        for q in range(AT_ONCE):
            ap = AT_ONCE * p + q
            pair = [
                rows_of([
                    flat[pl.ds((c * 2 + h) * 2 * pairs + ap * 2 + b, units, stride=8 * pairs), :]
                    for c in range(2) for b in range(2)
                ])
                for h in range(2)
            ]
            parts.append(in_order(*pair))
        y = apply(left, jnp.concatenate(parts, axis=1))
        for q in range(AT_ONCE):
            ap = AT_ONCE * p + q
            for c in range(2):
                pair = weave(
                    kept_ref[c, ap * GATE:(ap + 1) * GATE, :],
                    y[c * GATE:(c + 1) * GATE, q * LANES:(q + 1) * LANES],
                )
                for h in range(2):
                    out_ref[h, pl.ds(ap * 2 * GATE + c, GATE, stride=2), :] = pair[h]


def farthest_first(count):
    return [d for d in range(count // 2, count)] + [d for d in range(1, count // 2)]


def partner(me, distance, count):
    to, bit = 0, 1
    while bit < count:
        mine = lax.rem(lax.div(me, bit), 2)
        to = to + bit * (1 - mine if distance & bit else mine)
        bit *= 2
    return to


def kernel(narrow, wide, gates_hbm, roster_hbm, x_hbm, kept_hbm, mixed_hbm, last_hbm,
           gates_ref, roster_ref, x_ref, left_ref, plane, mixed, send_n, recv_n, send_w, recv_w,
           load_sem, x_sem, kept_sem, last_sem, mixed_sem, sent_n, came_n, sent_w, came_w):
    me_n, me_w = lax.axis_index("narrow"), lax.axis_index("wide")
    blocks = x_ref.shape[0] // (2 * GATE)
    half = blocks // 2
    chunks = half // PER_CHUNK
    rows_n, rows_w = GATE // narrow, GATE // wide
    split_rows = blocks * GATE
    block_rows = 2 * GATE

    loads = [
        pltpu.make_async_copy(roster_hbm, roster_ref, load_sem.at[0]),
        pltpu.make_async_copy(gates_hbm, gates_ref, load_sem.at[1]),
    ]
    for load in loads:
        load.start()
    piece = half // PIECES

    def x_load(p, h):
        rows = pl.ds(pl.multiple_of((h * half + p * piece) * block_rows, block_rows), piece * block_rows)
        return pltpu.make_async_copy(x_hbm.at[rows], x_ref.at[rows], x_sem.at[p, h])

    for p in range(PIECES):
        for h in range(2):
            x_load(p, h).start()

    barrier = pltpu.get_barrier_semaphore()

    def greet_n(d, _):
        pl.semaphore_signal(barrier, inc=1, device_id={"narrow": lax.rem(me_n + d, narrow)}, device_id_type=MESH)
        return 0

    def greet_w(d, _):
        pl.semaphore_signal(barrier, inc=1, device_id={"wide": lax.rem(me_w + d, wide)}, device_id_type=MESH)
        return 0

    lax.fori_loop(1, narrow, greet_n, 0)
    lax.fori_loop(1, wide, greet_w, 0)

    def bank(k):
        return block_of(gates_ref[roster_ref[k]])

    loads[0].wait()
    loads[1].wait()
    for i in range(2):
        left_ref[i] = left_of(bank(i))

    def keep(split, ap, y):
        for c in range(2):
            start = pl.multiple_of(split * split_rows + c * half * GATE + ap * GATE, GATE)
            plane[pl.ds(start, GATE), :] = y[c * GATE:(c + 1) * GATE]

    def first(split):
        def step(i, _):
            parts = []
            for q in range(AT_ONCE):
                pair = [
                    rows_of([x_ref[pl.ds(a * block_rows + c, GATE, stride=2), :] for c in range(2)])
                    for a in (AT_ONCE * i + q, AT_ONCE * i + q + half)
                ]
                parts.append(weave(*pair)[split])
            y = apply(left_ref[0], jnp.concatenate(parts, axis=1))
            for q in range(AT_ONCE):
                keep(split, AT_ONCE * i + q, y[:, q * LANES:(q + 1) * LANES])
            return 0

        def steps(p, _):
            if split == 0:
                for h in range(2):
                    x_load(p, h).wait()
            lax.fori_loop(p * (piece // AT_ONCE), (p + 1) * (piece // AT_ONCE), step, 0)
            return 0

        lax.fori_loop(0, PIECES, steps, 0)

    def second(phase, ch):
        rnd, split = phase // 2, phase % 2
        parts = []
        for q in range(PER_CHUNK):
            unit = ch * PER_CHUNK + q
            rows = []
            for c in range(2):
                base = split * split_rows + c * half * GATE + unit
                rows += weave(
                    plane[pl.ds(base, blocks, stride=blocks), :],
                    plane[pl.ds(base + half, blocks, stride=blocks), :],
                )
            parts.append(rows_of(rows))
        y = apply(left_ref[4 * rnd + 1], jnp.concatenate(parts, axis=1))
        for q in range(PER_CHUNK):
            for c in range(2):
                for n in range(narrow):
                    at = (q * 2 + c) * rows_n
                    send_n[phase, ch, n, at:at + rows_n, :] = y[
                        c * GATE + n * rows_n:c * GATE + (n + 1) * rows_n,
                        q * LANES:(q + 1) * LANES,
                    ]
        for d in farthest_first(narrow):
            to = partner(me_n, d, narrow)
            pltpu.make_async_remote_copy(
                src_ref=send_n.at[phase, ch, to],
                dst_ref=recv_n.at[phase, ch, me_n],
                send_sem=sent_n.at[phase, ch],
                recv_sem=came_n.at[phase, ch],
                device_id={"narrow": to},
                device_id_type=MESH,
            ).start()
        recv_n[phase, ch, me_n] = send_n[phase, ch, me_n]

    def third(phase, ch):
        rnd = phase // 2
        pltpu.make_async_copy(
            send_n.at[phase, ch, pl.ds(0, narrow - 1)],
            recv_n.at[phase, ch, pl.ds(0, narrow - 1)],
            came_n.at[phase, ch],
        ).wait()
        x = jnp.concatenate(
            [
                rows_of([
                    recv_n[phase, ch, n, pl.ds((q * 2 + c) * rows_n, rows_n), :]
                    for c in range(2) for n in range(narrow)
                ])
                for q in range(PER_CHUNK)
            ],
            axis=1,
        )
        y = apply(left_ref[4 * rnd + 2], x)
        for q in range(PER_CHUNK):
            for c in range(2):
                for w in range(wide):
                    at = (q * 2 + c) * rows_w
                    send_w[phase, ch, w, at:at + rows_w, :] = y[
                        c * GATE + w * rows_w:c * GATE + (w + 1) * rows_w,
                        q * LANES:(q + 1) * LANES,
                    ]

        def push(d, _):
            to = lax.rem(me_w + d, wide)
            pltpu.make_async_remote_copy(
                src_ref=send_w.at[phase, ch, to],
                dst_ref=recv_w.at[phase, ch, me_w],
                send_sem=sent_w.at[phase, ch],
                recv_sem=came_w.at[phase, ch],
                device_id={"wide": to},
                device_id_type=MESH,
            ).start()
            return 0

        lax.fori_loop(1, wide, push, 0, unroll=wide <= 8)
        recv_w[phase, ch, me_w] = send_w[phase, ch, me_w]

    def fourth(phase, ch):
        rnd, split = phase // 2, phase % 2
        pltpu.make_async_copy(
            send_w.at[phase, ch, pl.ds(0, wide - 1)],
            recv_w.at[phase, ch, pl.ds(0, wide - 1)],
            came_w.at[phase, ch],
        ).wait()
        x = jnp.concatenate(
            [
                rows_of([
                    recv_w[phase, ch, w, pl.ds((q * 2 + c) * rows_w, rows_w), :]
                    for c in range(2) for w in range(wide)
                ])
                for q in range(PER_CHUNK)
            ],
            axis=1,
        )
        y = apply(left_ref[4 * rnd + 3], x)
        for q in range(PER_CHUNK):
            unit = ch * PER_CHUNK + q
            start = pl.multiple_of(split * split_rows + unit * block_rows, block_rows)
            mixed[pl.ds(start, block_rows), :] = y[:, q * LANES:(q + 1) * LANES]

    def fifth(phase):
        rnd, split = phase // 2, phase % 2

        def step(i, _):
            parts = []
            for q in range(AT_ONCE):
                pair = [
                    rows_of([
                        mixed[pl.ds(split * split_rows + c * GATE + a * 2 + b, half, stride=block_rows), :]
                        for c in range(2) for b in range(2)
                    ])
                    for a in (AT_ONCE * i + q, AT_ONCE * i + q + half)
                ]
                parts.append(in_order(*pair))
            y = apply(left_ref[4 * rnd + 4], jnp.concatenate(parts, axis=1))
            for q in range(AT_ONCE):
                ap = AT_ONCE * i + q
                keep(split, ap, y[:, q * LANES:(q + 1) * LANES])
            return 0

        lax.fori_loop(0, half // AT_ONCE, step, 0)

    def over_chunks(body):
        def step(ch, _):
            body(ch)
            return 0

        lax.fori_loop(0, chunks, step, 0)

    first(0)
    pl.semaphore_wait(barrier, narrow - 1 + wide - 1)
    over_chunks(lambda ch: second(0, ch))
    first(1)
    for rnd in range(ROUNDS):
        for i in range(max(2 - 4 * rnd, 1), 4):
            if 4 * rnd + i > 1:
                left_ref[4 * rnd + i] = left_of(bank(5 * rnd + i))
        last = bank(5 * rnd + 4)
        if rnd < ROUNDS - 1:
            last = jnp.dot(
                bank(5 * rnd + 5), last, precision=lax.Precision.HIGHEST,
                preferred_element_type=jnp.float32,
            )
        left_ref[4 * rnd + 4] = left_of(last)

    last_out = pltpu.make_async_copy(left_ref.at[4 * ROUNDS], last_hbm, last_sem)
    last_out.start()
    kept_out = pltpu.make_async_copy(plane.at[pl.ds(0, split_rows)], kept_hbm, kept_sem)

    def mixed_out(ch):
        rows = PER_CHUNK * block_rows
        start = pl.multiple_of(ch * rows, rows)
        return pltpu.make_async_copy(
            mixed.at[pl.ds(split_rows + start, rows)], mixed_hbm.at[pl.ds(start, rows)], mixed_sem.at[ch]
        )

    def ending(ch):
        fourth(2 * ROUNDS - 1, ch)
        mixed_out(ch).start()

    for phase in range(2 * ROUNDS):
        def exchange(ch, phase=phase):
            third(phase, ch)
            if phase + 1 < 2 * ROUNDS:
                second(phase + 1, ch)

        over_chunks(exchange)
        if phase + 1 < 2 * ROUNDS:
            over_chunks(functools.partial(fourth, phase))
            fifth(phase)
            if phase == 2 * ROUNDS - 2:
                kept_out.start()
        else:
            over_chunks(ending)

    def settle(ch):
        for phase in range(2 * ROUNDS):
            pltpu.make_async_copy(
                send_n.at[phase, ch, pl.ds(0, narrow - 1)],
                recv_n.at[phase, ch, pl.ds(0, narrow - 1)],
                sent_n.at[phase, ch],
            ).wait()
            pltpu.make_async_copy(
                send_w.at[phase, ch, pl.ds(0, wide - 1)],
                recv_w.at[phase, ch, pl.ds(0, wide - 1)],
                sent_w.at[phase, ch],
            ).wait()

    over_chunks(settle)
    last_out.wait()
    kept_out.wait()
    over_chunks(lambda ch: mixed_out(ch).wait())


def on_device(state, gates, roster):
    narrow, wide = lax.axis_size("narrow"), lax.axis_size("wide")
    rows = state.shape[1] // LANES
    chunks = rows // GATE // 2 // PER_CHUNK
    phases = 2 * ROUNDS
    x = state.reshape(2, rows, LANES).transpose(1, 0, 2).reshape(2 * rows, LANES)
    f32 = jnp.float32
    trade_n = pltpu.VMEM((phases, chunks, narrow, PER_CHUNK * 2 * GATE // narrow, LANES), f32)
    trade_w = pltpu.VMEM((phases, chunks, wide, PER_CHUNK * 2 * GATE // wide, LANES), f32)
    dma = pltpu.SemaphoreType.DMA((phases, chunks))
    hbm = pl.BlockSpec(memory_space=pltpu.HBM)
    whole = pltpu.VMEM((2 * rows, LANES), f32)
    half_state = jax.ShapeDtypeStruct((rows, LANES), f32)
    factor = jax.ShapeDtypeStruct((4 * GATE, 4 * GATE), jnp.bfloat16)
    kept, mixed, last = pl.pallas_call(
        functools.partial(kernel, narrow, wide),
        out_shape=[half_state, half_state, factor],
        in_specs=[hbm, hbm, hbm],
        out_specs=[hbm, hbm, hbm],
        scratch_shapes=[
            pltpu.VMEM(gates.shape, f32),
            pltpu.SMEM(roster.shape, jnp.int32),
            whole,
            pltpu.VMEM((4 * ROUNDS + 1, 4 * GATE, 4 * GATE), jnp.bfloat16),
            whole, whole,
            trade_n, trade_n, trade_w, trade_w,
            pltpu.SemaphoreType.DMA((2,)),
            pltpu.SemaphoreType.DMA((PIECES, 2)),
            pltpu.SemaphoreType.DMA, pltpu.SemaphoreType.DMA,
            pltpu.SemaphoreType.DMA((chunks,)),
            dma, dma, dma, dma,
        ],
        compiler_params=pltpu.CompilerParams(
            collective_id=0, has_side_effects=True, vmem_limit_bytes=64 * 1024 * 1024
        ),
    )(gates, roster, x)

    half = rows // GATE // 2
    pairs = half // PIECES
    out = pl.pallas_call(
        closing,
        grid=(PIECES,),
        out_shape=jax.ShapeDtypeStruct((2, rows, LANES), f32),
        in_specs=[
            pl.BlockSpec((4 * GATE, 4 * GATE), lambda i: (0, 0)),
            pl.BlockSpec((2, pairs * GATE, LANES), lambda i: (0, i, 0)),
            pl.BlockSpec((half, 2, 2, 2 * pairs, LANES), lambda i: (0, 0, 0, i, 0)),
        ],
        out_specs=pl.BlockSpec((2, pairs * 2 * GATE, LANES), lambda i: (0, i, 0)),
        compiler_params=pltpu.CompilerParams(vmem_limit_bytes=64 * 1024 * 1024),
    )(last, kept.reshape(2, half * GATE, LANES), mixed.reshape(half, 2, 2, GATE // 2, LANES))
    return out.reshape(rows, 2, LANES).transpose(1, 0, 2).reshape(2, rows * LANES)


def solution(mesh):
    in_specs = (P(None, ("wide", "narrow")), P(), P())
    out_specs = P(None, ("wide", "narrow"))
    return jax.shard_map(
        on_device, mesh=mesh, in_specs=in_specs, out_specs=out_specs, check_vma=False
    )
```

```python
import functools

import jax
import jax.numpy as jnp
from jax import lax
from jax.experimental import pallas as pl
from jax.experimental.pallas import tpu as pltpu
from jax.sharding import PartitionSpec as P

ROUNDS = 2
GATE = 64
LANES = 128
PER_CHUNK = 4
PIECES = 4
AT_ONCE = 4
STEPS = 2
MESH = pl.DeviceIdType.MESH


def block_of(gate):
    re, im = gate[0], gate[1]
    top = jnp.concatenate([re, -im], axis=1)
    bottom = jnp.concatenate([im, re], axis=1)
    return jnp.concatenate([top, bottom], axis=0)


def halves(value):
    high = value.astype(jnp.bfloat16)
    return high, (value - high.astype(jnp.float32)).astype(jnp.bfloat16)


def left_of(block):
    high, low = halves(block)
    top = jnp.concatenate([high, high], axis=1)
    bottom = jnp.concatenate([low, jnp.zeros_like(low)], axis=1)
    return jnp.concatenate([top, bottom], axis=0)


def apply(left, amps):
    high, low = halves(amps)
    out = jnp.dot(
        left, jnp.concatenate([high, low], axis=0), preferred_element_type=jnp.float32
    )
    return out[: 2 * GATE] + out[2 * GATE :]


def weave(first, second):
    low = lax.broadcasted_iota(jnp.int32, first.shape, 1) < LANES // 2
    turned_first = pltpu.roll(first, LANES // 2, 1)
    turned_second = pltpu.roll(second, LANES // 2, 1)
    return jnp.where(low, first, turned_second), jnp.where(low, turned_first, second)


def rows_of(parts):
    return jnp.concatenate(parts, axis=0)


def in_order(first, second):
    lower, upper = weave(first, second)
    half = first.shape[0] // 4
    rows = []
    for k in range(4):
        rows += [lower[k * half:(k + 1) * half], upper[k * half:(k + 1) * half]]
    return rows_of(rows)


def closing(left_ref, kept_ref, mixed_ref, out_ref):
    units, pairs = mixed_ref.shape[0], kept_ref.shape[1] // GATE
    flat = mixed_ref.reshape(units * 4 * 2 * pairs, LANES)
    left = left_ref[...]
    for p in range(pairs // AT_ONCE):
        parts = []
        for q in range(AT_ONCE):
            ap = AT_ONCE * p + q
            pair = [
                rows_of([
                    flat[pl.ds((c * 2 + h) * 2 * pairs + ap * 2 + b, units, stride=8 * pairs), :]
                    for c in range(2) for b in range(2)
                ])
                for h in range(2)
            ]
            parts.append(in_order(*pair))
        y = apply(left, jnp.concatenate(parts, axis=1))
        for q in range(AT_ONCE):
            ap = AT_ONCE * p + q
            for c in range(2):
                pair = weave(
                    kept_ref[c, ap * GATE:(ap + 1) * GATE, :],
                    y[c * GATE:(c + 1) * GATE, q * LANES:(q + 1) * LANES],
                )
                for h in range(2):
                    out_ref[h, pl.ds(ap * 2 * GATE + c, GATE, stride=2), :] = pair[h]


def kernel(narrow, wide, gates_hbm, roster_hbm, x_hbm, kept_hbm, mixed_hbm, last_hbm,
           gates_ref, roster_ref, x_ref, left_ref, plane, mixed, send_n, recv_n, send_w, recv_w,
           load_sem, x_sem, kept_sem, last_sem, mixed_sem, sent_n, came_n, sent_w, came_w):
    me_n, me_w = lax.axis_index("narrow"), lax.axis_index("wide")
    blocks = x_ref.shape[0] // (2 * GATE)
    half = blocks // 2
    chunks = half // PER_CHUNK
    rows_n, rows_w = GATE // narrow, GATE // wide
    split_rows = blocks * GATE
    block_rows = 2 * GATE

    loads = [
        pltpu.make_async_copy(roster_hbm, roster_ref, load_sem.at[0]),
        pltpu.make_async_copy(gates_hbm, gates_ref, load_sem.at[1]),
    ]
    for load in loads:
        load.start()
    piece = half // PIECES

    def x_load(p, h):
        rows = pl.ds(pl.multiple_of((h * half + p * piece) * block_rows, block_rows), piece * block_rows)
        return pltpu.make_async_copy(x_hbm.at[rows], x_ref.at[rows], x_sem.at[p, h])

    for p in range(PIECES):
        for h in range(2):
            x_load(p, h).start()

    barrier = pltpu.get_barrier_semaphore()

    def greet_n(d, _):
        pl.semaphore_signal(barrier, inc=1, device_id={"narrow": lax.rem(me_n + d, narrow)}, device_id_type=MESH)
        return 0

    def greet_w(d, _):
        pl.semaphore_signal(barrier, inc=1, device_id={"wide": lax.rem(me_w + d, wide)}, device_id_type=MESH)
        return 0

    lax.fori_loop(1, narrow, greet_n, 0)
    lax.fori_loop(1, wide, greet_w, 0)

    def bank(k):
        return block_of(gates_ref[roster_ref[k]])

    loads[0].wait()
    loads[1].wait()
    for i in range(2):
        left_ref[i] = left_of(bank(i))

    def keep(split, ap, y):
        for c in range(2):
            start = pl.multiple_of(split * split_rows + c * half * GATE + ap * GATE, GATE)
            plane[pl.ds(start, GATE), :] = y[c * GATE:(c + 1) * GATE]

    def first(split):
        def step(i, _):
            parts = []
            for q in range(AT_ONCE):
                pair = [
                    rows_of([x_ref[pl.ds(a * block_rows + c, GATE, stride=2), :] for c in range(2)])
                    for a in (AT_ONCE * i + q, AT_ONCE * i + q + half)
                ]
                parts.append(weave(*pair)[split])
            y = apply(left_ref[0], jnp.concatenate(parts, axis=1))
            for q in range(AT_ONCE):
                keep(split, AT_ONCE * i + q, y[:, q * LANES:(q + 1) * LANES])
            return 0

        def steps(p, _):
            if split == 0:
                for h in range(2):
                    x_load(p, h).wait()
            lax.fori_loop(p * (piece // AT_ONCE), (p + 1) * (piece // AT_ONCE), step, 0)
            return 0

        lax.fori_loop(0, PIECES, steps, 0)

    def second(phase, ch):
        rnd, split = phase // 2, phase % 2
        parts = []
        for q in range(PER_CHUNK):
            unit = ch * PER_CHUNK + q
            rows = []
            for c in range(2):
                base = split * split_rows + c * half * GATE + unit
                rows += weave(
                    plane[pl.ds(base, blocks, stride=blocks), :],
                    plane[pl.ds(base + half, blocks, stride=blocks), :],
                )
            parts.append(rows_of(rows))
        y = apply(left_ref[4 * rnd + 1], jnp.concatenate(parts, axis=1))
        for q in range(PER_CHUNK):
            for c in range(2):
                for n in range(narrow):
                    at = (q * 2 + c) * rows_n
                    send_n[phase, ch, n, at:at + rows_n, :] = y[
                        c * GATE + n * rows_n:c * GATE + (n + 1) * rows_n,
                        q * LANES:(q + 1) * LANES,
                    ]
        for d in range(1, narrow):
            to = lax.rem(me_n + lax.rem(me_w, 2) * (narrow - 2 * d) + d, narrow)
            pltpu.make_async_remote_copy(
                src_ref=send_n.at[phase, ch, to],
                dst_ref=recv_n.at[phase, ch, me_n],
                send_sem=sent_n.at[phase, ch],
                recv_sem=came_n.at[phase, ch],
                device_id={"narrow": to},
                device_id_type=MESH,
            ).start()
        recv_n[phase, ch, me_n] = send_n[phase, ch, me_n]

    def third(phase, ch):
        rnd = phase // 2
        pltpu.make_async_copy(
            send_n.at[phase, ch, pl.ds(0, narrow - 1)],
            recv_n.at[phase, ch, pl.ds(0, narrow - 1)],
            came_n.at[phase, ch],
        ).wait()
        x = jnp.concatenate(
            [
                rows_of([
                    recv_n[phase, ch, n, pl.ds((q * 2 + c) * rows_n, rows_n), :]
                    for c in range(2) for n in range(narrow)
                ])
                for q in range(PER_CHUNK)
            ],
            axis=1,
        )
        y = apply(left_ref[4 * rnd + 2], x)
        for q in range(PER_CHUNK):
            for c in range(2):
                for w in range(wide):
                    at = (q * 2 + c) * rows_w
                    send_w[phase, ch, w, at:at + rows_w, :] = y[
                        c * GATE + w * rows_w:c * GATE + (w + 1) * rows_w,
                        q * LANES:(q + 1) * LANES,
                    ]

        def push(d, _):
            to = lax.rem(me_w + d, wide)
            pltpu.make_async_remote_copy(
                src_ref=send_w.at[phase, ch, to],
                dst_ref=recv_w.at[phase, ch, me_w],
                send_sem=sent_w.at[phase, ch],
                recv_sem=came_w.at[phase, ch],
                device_id={"wide": to},
                device_id_type=MESH,
            ).start()
            return 0

        lax.fori_loop(1, wide, push, 0, unroll=wide <= 8)
        recv_w[phase, ch, me_w] = send_w[phase, ch, me_w]

    def fourth(phase, ch):
        rnd, split = phase // 2, phase % 2
        pltpu.make_async_copy(
            send_w.at[phase, ch, pl.ds(0, wide - 1)],
            recv_w.at[phase, ch, pl.ds(0, wide - 1)],
            came_w.at[phase, ch],
        ).wait()
        x = jnp.concatenate(
            [
                rows_of([
                    recv_w[phase, ch, w, pl.ds((q * 2 + c) * rows_w, rows_w), :]
                    for c in range(2) for w in range(wide)
                ])
                for q in range(PER_CHUNK)
            ],
            axis=1,
        )
        y = apply(left_ref[4 * rnd + 3], x)
        for q in range(PER_CHUNK):
            unit = ch * PER_CHUNK + q
            start = pl.multiple_of(split * split_rows + unit * block_rows, block_rows)
            mixed[pl.ds(start, block_rows), :] = y[:, q * LANES:(q + 1) * LANES]

    def fifth(phase):
        rnd, split = phase // 2, phase % 2

        def step(i, _):
            parts = []
            for q in range(AT_ONCE):
                pair = [
                    rows_of([
                        mixed[pl.ds(split * split_rows + c * GATE + a * 2 + b, half, stride=block_rows), :]
                        for c in range(2) for b in range(2)
                    ])
                    for a in (AT_ONCE * i + q, AT_ONCE * i + q + half)
                ]
                parts.append(in_order(*pair))
            y = apply(left_ref[4 * rnd + 4], jnp.concatenate(parts, axis=1))
            for q in range(AT_ONCE):
                ap = AT_ONCE * i + q
                keep(split, ap, y[:, q * LANES:(q + 1) * LANES])
            return 0

        lax.fori_loop(0, half // AT_ONCE, step, 0)

    def over_chunks(body):
        def step(ch, _):
            body(ch)
            return 0

        lax.fori_loop(0, chunks, step, 0)

    first(0)
    pl.semaphore_wait(barrier, narrow - 1 + wide - 1)
    over_chunks(lambda ch: second(0, ch))
    first(1)
    for rnd in range(ROUNDS):
        for i in range(max(2 - 4 * rnd, 1), 4):
            if 4 * rnd + i > 1:
                left_ref[4 * rnd + i] = left_of(bank(5 * rnd + i))
        last = bank(5 * rnd + 4)
        if rnd < ROUNDS - 1:
            last = jnp.dot(
                bank(5 * rnd + 5), last, precision=lax.Precision.HIGHEST,
                preferred_element_type=jnp.float32,
            )
        left_ref[4 * rnd + 4] = left_of(last)

    last_out = pltpu.make_async_copy(left_ref.at[4 * ROUNDS], last_hbm, last_sem)
    last_out.start()
    kept_out = pltpu.make_async_copy(plane.at[pl.ds(0, split_rows)], kept_hbm, kept_sem)

    def mixed_out(ch):
        rows = PER_CHUNK * block_rows
        start = pl.multiple_of(ch * rows, rows)
        return pltpu.make_async_copy(
            mixed.at[pl.ds(split_rows + start, rows)], mixed_hbm.at[pl.ds(start, rows)], mixed_sem.at[ch]
        )

    def ending(ch):
        fourth(2 * ROUNDS - 1, ch)
        mixed_out(ch).start()

    for phase in range(2 * ROUNDS):
        def exchange(ch, phase=phase):
            third(phase, ch)
            if phase + 1 < 2 * ROUNDS:
                second(phase + 1, ch)

        over_chunks(exchange)
        if phase + 1 < 2 * ROUNDS:
            over_chunks(functools.partial(fourth, phase))
            fifth(phase)
            if phase == 2 * ROUNDS - 2:
                kept_out.start()
        else:
            over_chunks(ending)

    def settle(ch):
        for phase in range(2 * ROUNDS):
            pltpu.make_async_copy(
                send_n.at[phase, ch, pl.ds(0, narrow - 1)],
                recv_n.at[phase, ch, pl.ds(0, narrow - 1)],
                sent_n.at[phase, ch],
            ).wait()
            pltpu.make_async_copy(
                send_w.at[phase, ch, pl.ds(0, wide - 1)],
                recv_w.at[phase, ch, pl.ds(0, wide - 1)],
                sent_w.at[phase, ch],
            ).wait()

    over_chunks(settle)
    last_out.wait()
    kept_out.wait()
    over_chunks(lambda ch: mixed_out(ch).wait())


def on_device(state, gates, roster):
    narrow, wide = lax.axis_size("narrow"), lax.axis_size("wide")
    rows = state.shape[1] // LANES
    chunks = rows // GATE // 2 // PER_CHUNK
    phases = 2 * ROUNDS
    x = state.reshape(2, rows, LANES).transpose(1, 0, 2).reshape(2 * rows, LANES)
    f32 = jnp.float32
    trade_n = pltpu.VMEM((phases, chunks, narrow, PER_CHUNK * 2 * GATE // narrow, LANES), f32)
    trade_w = pltpu.VMEM((phases, chunks, wide, PER_CHUNK * 2 * GATE // wide, LANES), f32)
    dma = pltpu.SemaphoreType.DMA((phases, chunks))
    hbm = pl.BlockSpec(memory_space=pltpu.HBM)
    whole = pltpu.VMEM((2 * rows, LANES), f32)
    half_state = jax.ShapeDtypeStruct((rows, LANES), f32)
    factor = jax.ShapeDtypeStruct((4 * GATE, 4 * GATE), jnp.bfloat16)
    kept, mixed, last = pl.pallas_call(
        functools.partial(kernel, narrow, wide),
        out_shape=[half_state, half_state, factor],
        in_specs=[hbm, hbm, hbm],
        out_specs=[hbm, hbm, hbm],
        scratch_shapes=[
            pltpu.VMEM(gates.shape, f32),
            pltpu.SMEM(roster.shape, jnp.int32),
            whole,
            pltpu.VMEM((4 * ROUNDS + 1, 4 * GATE, 4 * GATE), jnp.bfloat16),
            whole, whole,
            trade_n, trade_n, trade_w, trade_w,
            pltpu.SemaphoreType.DMA((2,)),
            pltpu.SemaphoreType.DMA((PIECES, 2)),
            pltpu.SemaphoreType.DMA, pltpu.SemaphoreType.DMA,
            pltpu.SemaphoreType.DMA((chunks,)),
            dma, dma, dma, dma,
        ],
        compiler_params=pltpu.CompilerParams(
            collective_id=0, has_side_effects=True, vmem_limit_bytes=64 * 1024 * 1024
        ),
    )(gates, roster, x)

    half = rows // GATE // 2
    pairs = half // STEPS
    out = pl.pallas_call(
        closing,
        grid=(STEPS,),
        out_shape=jax.ShapeDtypeStruct((2, rows, LANES), f32),
        in_specs=[
            pl.BlockSpec((4 * GATE, 4 * GATE), lambda i: (0, 0)),
            pl.BlockSpec((2, pairs * GATE, LANES), lambda i: (0, i, 0)),
            pl.BlockSpec((half, 2, 2, 2 * pairs, LANES), lambda i: (0, 0, 0, i, 0)),
        ],
        out_specs=pl.BlockSpec((2, pairs * 2 * GATE, LANES), lambda i: (0, i, 0)),
        compiler_params=pltpu.CompilerParams(vmem_limit_bytes=64 * 1024 * 1024),
    )(last, kept.reshape(2, half * GATE, LANES), mixed.reshape(half, 2, 2, GATE // 2, LANES))
    return out.reshape(rows, 2, LANES).transpose(1, 0, 2).reshape(2, rows * LANES)


def solution(mesh):
    in_specs = (P(None, ("wide", "narrow")), P(), P())
    out_specs = P(None, ("wide", "narrow"))
    return jax.shard_map(
        on_device, mesh=mesh, in_specs=in_specs, out_specs=out_specs, check_vma=False
    )
```

```python
import functools

import jax
import jax.numpy as jnp
from jax import lax
from jax.experimental import pallas as pl
from jax.experimental.pallas import tpu as pltpu
from jax.sharding import PartitionSpec as P

ROUNDS = 2
GATE = 64
LANES = 128
PER_CHUNK = 4
PIECES = 4
AT_ONCE = 4
STEPS = 2
MESH = pl.DeviceIdType.MESH


def block_of(gate):
    re, im = gate[0], gate[1]
    top = jnp.concatenate([re, -im], axis=1)
    bottom = jnp.concatenate([im, re], axis=1)
    return jnp.concatenate([top, bottom], axis=0)


def halves(value):
    high = value.astype(jnp.bfloat16)
    return high, (value - high.astype(jnp.float32)).astype(jnp.bfloat16)


def left_of(block):
    high, low = halves(block)
    top = jnp.concatenate([high, high], axis=1)
    bottom = jnp.concatenate([low, jnp.zeros_like(low)], axis=1)
    return jnp.concatenate([top, bottom], axis=0)


def apply(left, amps):
    high, low = halves(amps)
    out = jnp.dot(
        left, jnp.concatenate([high, low], axis=0), preferred_element_type=jnp.float32
    )
    return out[: 2 * GATE] + out[2 * GATE :]


def weave(first, second):
    low = lax.broadcasted_iota(jnp.int32, first.shape, 1) < LANES // 2
    turned_first = pltpu.roll(first, LANES // 2, 1)
    turned_second = pltpu.roll(second, LANES // 2, 1)
    return jnp.where(low, first, turned_second), jnp.where(low, turned_first, second)


def rows_of(parts):
    return jnp.concatenate(parts, axis=0)


def in_order(first, second):
    lower, upper = weave(first, second)
    half = first.shape[0] // 4
    rows = []
    for k in range(4):
        rows += [lower[k * half:(k + 1) * half], upper[k * half:(k + 1) * half]]
    return rows_of(rows)


def closing(left_ref, kept_ref, mixed_ref, out_ref):
    units, pairs = mixed_ref.shape[0], kept_ref.shape[1] // GATE
    flat = mixed_ref.reshape(units * 4 * 2 * pairs, LANES)
    left = left_ref[...]
    for p in range(pairs // AT_ONCE):
        parts = []
        for q in range(AT_ONCE):
            ap = AT_ONCE * p + q
            pair = [
                rows_of([
                    flat[pl.ds((c * 2 + h) * 2 * pairs + ap * 2 + b, units, stride=8 * pairs), :]
                    for c in range(2) for b in range(2)
                ])
                for h in range(2)
            ]
            parts.append(in_order(*pair))
        y = apply(left, jnp.concatenate(parts, axis=1))
        for q in range(AT_ONCE):
            ap = AT_ONCE * p + q
            for c in range(2):
                pair = weave(
                    kept_ref[c, ap * GATE:(ap + 1) * GATE, :],
                    y[c * GATE:(c + 1) * GATE, q * LANES:(q + 1) * LANES],
                )
                for h in range(2):
                    out_ref[h, pl.ds(ap * 2 * GATE + c, GATE, stride=2), :] = pair[h]


def kernel(narrow, wide, gates_hbm, roster_hbm, x_hbm, kept_hbm, mixed_hbm, last_hbm,
           gates_ref, roster_ref, x_ref, left_ref, plane, mixed, send_n, recv_n, send_w, recv_w,
           load_sem, x_sem, kept_sem, last_sem, mixed_sem, sent_n, came_n, sent_w, came_w):
    me_n, me_w = lax.axis_index("narrow"), lax.axis_index("wide")
    blocks = x_ref.shape[0] // (2 * GATE)
    half = blocks // 2
    chunks = half // PER_CHUNK
    rows_n, rows_w = GATE // narrow, GATE // wide
    split_rows = blocks * GATE
    block_rows = 2 * GATE

    loads = [
        pltpu.make_async_copy(roster_hbm, roster_ref, load_sem.at[0]),
        pltpu.make_async_copy(gates_hbm, gates_ref, load_sem.at[1]),
    ]
    for load in loads:
        load.start()
    piece = half // PIECES

    def x_load(p, h):
        rows = pl.ds(pl.multiple_of((h * half + p * piece) * block_rows, block_rows), piece * block_rows)
        return pltpu.make_async_copy(x_hbm.at[rows], x_ref.at[rows], x_sem.at[p, h])

    for p in range(PIECES):
        for h in range(2):
            x_load(p, h).start()

    barrier = pltpu.get_barrier_semaphore()

    def greet_n(d, _):
        pl.semaphore_signal(barrier, inc=1, device_id={"narrow": lax.rem(me_n + d, narrow)}, device_id_type=MESH)
        return 0

    def greet_w(d, _):
        pl.semaphore_signal(barrier, inc=1, device_id={"wide": lax.rem(me_w + d, wide)}, device_id_type=MESH)
        return 0

    lax.fori_loop(1, narrow, greet_n, 0)
    lax.fori_loop(1, wide, greet_w, 0)

    def bank(k):
        return block_of(gates_ref[roster_ref[k]])

    loads[0].wait()
    loads[1].wait()
    for i in range(2):
        left_ref[i] = left_of(bank(i))

    def keep(split, ap, y):
        for c in range(2):
            start = pl.multiple_of(split * split_rows + c * half * GATE + ap * GATE, GATE)
            plane[pl.ds(start, GATE), :] = y[c * GATE:(c + 1) * GATE]

    def first(split):
        def step(i, _):
            parts = []
            for q in range(AT_ONCE):
                pair = [
                    rows_of([x_ref[pl.ds(a * block_rows + c, GATE, stride=2), :] for c in range(2)])
                    for a in (AT_ONCE * i + q, AT_ONCE * i + q + half)
                ]
                parts.append(weave(*pair)[split])
            y = apply(left_ref[0], jnp.concatenate(parts, axis=1))
            for q in range(AT_ONCE):
                keep(split, AT_ONCE * i + q, y[:, q * LANES:(q + 1) * LANES])
            return 0

        def steps(p, _):
            if split == 0:
                for h in range(2):
                    x_load(p, h).wait()
            lax.fori_loop(p * (piece // AT_ONCE), (p + 1) * (piece // AT_ONCE), step, 0)
            return 0

        lax.fori_loop(0, PIECES, steps, 0)

    def second(phase, ch):
        rnd, split = phase // 2, phase % 2
        parts = []
        for q in range(PER_CHUNK):
            unit = ch * PER_CHUNK + q
            rows = []
            for c in range(2):
                base = split * split_rows + c * half * GATE + unit
                rows += weave(
                    plane[pl.ds(base, blocks, stride=blocks), :],
                    plane[pl.ds(base + half, blocks, stride=blocks), :],
                )
            parts.append(rows_of(rows))
        y = apply(left_ref[4 * rnd + 1], jnp.concatenate(parts, axis=1))
        for q in range(PER_CHUNK):
            for c in range(2):
                for n in range(narrow):
                    at = (q * 2 + c) * rows_n
                    send_n[phase, ch, n, at:at + rows_n, :] = y[
                        c * GATE + n * rows_n:c * GATE + (n + 1) * rows_n,
                        q * LANES:(q + 1) * LANES,
                    ]
        back = lax.rem(me_w, 2) * lax.rem(ch, 2)
        for d in range(1, narrow):
            to = lax.rem(me_n + back * (narrow - 2 * d) + d, narrow)
            pltpu.make_async_remote_copy(
                src_ref=send_n.at[phase, ch, to],
                dst_ref=recv_n.at[phase, ch, me_n],
                send_sem=sent_n.at[phase, ch],
                recv_sem=came_n.at[phase, ch],
                device_id={"narrow": to},
                device_id_type=MESH,
            ).start()
        recv_n[phase, ch, me_n] = send_n[phase, ch, me_n]

    def third(phase, ch):
        rnd = phase // 2
        pltpu.make_async_copy(
            send_n.at[phase, ch, pl.ds(0, narrow - 1)],
            recv_n.at[phase, ch, pl.ds(0, narrow - 1)],
            came_n.at[phase, ch],
        ).wait()
        x = jnp.concatenate(
            [
                rows_of([
                    recv_n[phase, ch, n, pl.ds((q * 2 + c) * rows_n, rows_n), :]
                    for c in range(2) for n in range(narrow)
                ])
                for q in range(PER_CHUNK)
            ],
            axis=1,
        )
        y = apply(left_ref[4 * rnd + 2], x)
        for q in range(PER_CHUNK):
            for c in range(2):
                for w in range(wide):
                    at = (q * 2 + c) * rows_w
                    send_w[phase, ch, w, at:at + rows_w, :] = y[
                        c * GATE + w * rows_w:c * GATE + (w + 1) * rows_w,
                        q * LANES:(q + 1) * LANES,
                    ]

        def push(d, _):
            to = lax.rem(me_w + d, wide)
            pltpu.make_async_remote_copy(
                src_ref=send_w.at[phase, ch, to],
                dst_ref=recv_w.at[phase, ch, me_w],
                send_sem=sent_w.at[phase, ch],
                recv_sem=came_w.at[phase, ch],
                device_id={"wide": to},
                device_id_type=MESH,
            ).start()
            return 0

        lax.fori_loop(1, wide, push, 0, unroll=wide <= 8)
        recv_w[phase, ch, me_w] = send_w[phase, ch, me_w]

    def fourth(phase, ch):
        rnd, split = phase // 2, phase % 2
        pltpu.make_async_copy(
            send_w.at[phase, ch, pl.ds(0, wide - 1)],
            recv_w.at[phase, ch, pl.ds(0, wide - 1)],
            came_w.at[phase, ch],
        ).wait()
        x = jnp.concatenate(
            [
                rows_of([
                    recv_w[phase, ch, w, pl.ds((q * 2 + c) * rows_w, rows_w), :]
                    for c in range(2) for w in range(wide)
                ])
                for q in range(PER_CHUNK)
            ],
            axis=1,
        )
        y = apply(left_ref[4 * rnd + 3], x)
        for q in range(PER_CHUNK):
            unit = ch * PER_CHUNK + q
            start = pl.multiple_of(split * split_rows + unit * block_rows, block_rows)
            mixed[pl.ds(start, block_rows), :] = y[:, q * LANES:(q + 1) * LANES]

    def fifth(phase):
        rnd, split = phase // 2, phase % 2

        def step(i, _):
            parts = []
            for q in range(AT_ONCE):
                pair = [
                    rows_of([
                        mixed[pl.ds(split * split_rows + c * GATE + a * 2 + b, half, stride=block_rows), :]
                        for c in range(2) for b in range(2)
                    ])
                    for a in (AT_ONCE * i + q, AT_ONCE * i + q + half)
                ]
                parts.append(in_order(*pair))
            y = apply(left_ref[4 * rnd + 4], jnp.concatenate(parts, axis=1))
            for q in range(AT_ONCE):
                ap = AT_ONCE * i + q
                keep(split, ap, y[:, q * LANES:(q + 1) * LANES])
            return 0

        lax.fori_loop(0, half // AT_ONCE, step, 0)

    def over_chunks(body):
        def step(ch, _):
            body(ch)
            return 0

        lax.fori_loop(0, chunks, step, 0)

    first(0)
    pl.semaphore_wait(barrier, narrow - 1 + wide - 1)
    over_chunks(lambda ch: second(0, ch))
    first(1)
    for rnd in range(ROUNDS):
        for i in range(max(2 - 4 * rnd, 1), 4):
            if 4 * rnd + i > 1:
                left_ref[4 * rnd + i] = left_of(bank(5 * rnd + i))
        last = bank(5 * rnd + 4)
        if rnd < ROUNDS - 1:
            last = jnp.dot(
                bank(5 * rnd + 5), last, precision=lax.Precision.HIGHEST,
                preferred_element_type=jnp.float32,
            )
        left_ref[4 * rnd + 4] = left_of(last)

    last_out = pltpu.make_async_copy(left_ref.at[4 * ROUNDS], last_hbm, last_sem)
    last_out.start()
    kept_out = pltpu.make_async_copy(plane.at[pl.ds(0, split_rows)], kept_hbm, kept_sem)

    def mixed_out(ch):
        rows = PER_CHUNK * block_rows
        start = pl.multiple_of(ch * rows, rows)
        return pltpu.make_async_copy(
            mixed.at[pl.ds(split_rows + start, rows)], mixed_hbm.at[pl.ds(start, rows)], mixed_sem.at[ch]
        )

    def ending(ch):
        fourth(2 * ROUNDS - 1, ch)
        mixed_out(ch).start()

    def settle(phases, ch):
        for phase in phases:
            pltpu.make_async_copy(
                send_n.at[phase, ch, pl.ds(0, narrow - 1)],
                recv_n.at[phase, ch, pl.ds(0, narrow - 1)],
                sent_n.at[phase, ch],
            ).wait()
            pltpu.make_async_copy(
                send_w.at[phase, ch, pl.ds(0, wide - 1)],
                recv_w.at[phase, ch, pl.ds(0, wide - 1)],
                sent_w.at[phase, ch],
            ).wait()

    for phase in range(2 * ROUNDS):
        def exchange(ch, phase=phase):
            third(phase, ch)
            if phase + 1 < 2 * ROUNDS:
                second(phase + 1, ch)

        over_chunks(exchange)
        if phase + 1 < 2 * ROUNDS:
            over_chunks(functools.partial(fourth, phase))
            fifth(phase)
            if phase == 2 * ROUNDS - 2:
                kept_out.start()
                over_chunks(functools.partial(settle, range(2 * ROUNDS - 1)))
        else:
            over_chunks(ending)

    over_chunks(functools.partial(settle, [2 * ROUNDS - 1]))
    last_out.wait()
    kept_out.wait()
    over_chunks(lambda ch: mixed_out(ch).wait())


def on_device(state, gates, roster):
    narrow, wide = lax.axis_size("narrow"), lax.axis_size("wide")
    rows = state.shape[1] // LANES
    chunks = rows // GATE // 2 // PER_CHUNK
    phases = 2 * ROUNDS
    x = state.reshape(2, rows, LANES).transpose(1, 0, 2).reshape(2 * rows, LANES)
    f32 = jnp.float32
    trade_n = pltpu.VMEM((phases, chunks, narrow, PER_CHUNK * 2 * GATE // narrow, LANES), f32)
    trade_w = pltpu.VMEM((phases, chunks, wide, PER_CHUNK * 2 * GATE // wide, LANES), f32)
    dma = pltpu.SemaphoreType.DMA((phases, chunks))
    hbm = pl.BlockSpec(memory_space=pltpu.HBM)
    whole = pltpu.VMEM((2 * rows, LANES), f32)
    half_state = jax.ShapeDtypeStruct((rows, LANES), f32)
    factor = jax.ShapeDtypeStruct((4 * GATE, 4 * GATE), jnp.bfloat16)
    kept, mixed, last = pl.pallas_call(
        functools.partial(kernel, narrow, wide),
        out_shape=[half_state, half_state, factor],
        in_specs=[hbm, hbm, hbm],
        out_specs=[hbm, hbm, hbm],
        scratch_shapes=[
            pltpu.VMEM(gates.shape, f32),
            pltpu.SMEM(roster.shape, jnp.int32),
            whole,
            pltpu.VMEM((4 * ROUNDS + 1, 4 * GATE, 4 * GATE), jnp.bfloat16),
            whole, whole,
            trade_n, trade_n, trade_w, trade_w,
            pltpu.SemaphoreType.DMA((2,)),
            pltpu.SemaphoreType.DMA((PIECES, 2)),
            pltpu.SemaphoreType.DMA, pltpu.SemaphoreType.DMA,
            pltpu.SemaphoreType.DMA((chunks,)),
            dma, dma, dma, dma,
        ],
        compiler_params=pltpu.CompilerParams(
            collective_id=0, has_side_effects=True, vmem_limit_bytes=64 * 1024 * 1024
        ),
    )(gates, roster, x)

    half = rows // GATE // 2
    pairs = half // STEPS
    out = pl.pallas_call(
        closing,
        grid=(STEPS,),
        out_shape=jax.ShapeDtypeStruct((2, rows, LANES), f32),
        in_specs=[
            pl.BlockSpec((4 * GATE, 4 * GATE), lambda i: (0, 0)),
            pl.BlockSpec((2, pairs * GATE, LANES), lambda i: (0, i, 0)),
            pl.BlockSpec((half, 2, 2, 2 * pairs, LANES), lambda i: (0, 0, 0, i, 0)),
        ],
        out_specs=pl.BlockSpec((2, pairs * 2 * GATE, LANES), lambda i: (0, i, 0)),
        compiler_params=pltpu.CompilerParams(vmem_limit_bytes=64 * 1024 * 1024),
    )(last, kept.reshape(2, half * GATE, LANES), mixed.reshape(half, 2, 2, GATE // 2, LANES))
    return out.reshape(rows, 2, LANES).transpose(1, 0, 2).reshape(2, rows * LANES)


def solution(mesh):
    in_specs = (P(None, ("wide", "narrow")), P(), P())
    out_specs = P(None, ("wide", "narrow"))
    return jax.shard_map(
        on_device, mesh=mesh, in_specs=in_specs, out_specs=out_specs, check_vma=False
    )
```

```python
import functools

import jax
import jax.numpy as jnp
from jax import lax
from jax.experimental import pallas as pl
from jax.experimental.pallas import tpu as pltpu
from jax.sharding import PartitionSpec as P

ROUNDS = 2
GATE = 64
LANES = 128
PER_CHUNK = 4
PIECES = 4
AT_ONCE = 4
STEPS = 2
MESH = pl.DeviceIdType.MESH


def block_of(gate):
    re, im = gate[0], gate[1]
    top = jnp.concatenate([re, -im], axis=1)
    bottom = jnp.concatenate([im, re], axis=1)
    return jnp.concatenate([top, bottom], axis=0)


def halves(value):
    high = value.astype(jnp.bfloat16)
    return high, (value - high.astype(jnp.float32)).astype(jnp.bfloat16)


def left_of(block):
    high, low = halves(block)
    top = jnp.concatenate([high, high], axis=1)
    bottom = jnp.concatenate([low, jnp.zeros_like(low)], axis=1)
    return jnp.concatenate([top, bottom], axis=0)


def apply(left, amps):
    high, low = halves(amps)
    out = jnp.dot(
        left, jnp.concatenate([high, low], axis=0), preferred_element_type=jnp.float32
    )
    return out[: 2 * GATE] + out[2 * GATE :]


def weave(first, second):
    low = lax.broadcasted_iota(jnp.int32, first.shape, 1) < LANES // 2
    turned_first = pltpu.roll(first, LANES // 2, 1)
    turned_second = pltpu.roll(second, LANES // 2, 1)
    return jnp.where(low, first, turned_second), jnp.where(low, turned_first, second)


def rows_of(parts):
    return jnp.concatenate(parts, axis=0)


def in_order(first, second):
    lower, upper = weave(first, second)
    half = first.shape[0] // 4
    rows = []
    for k in range(4):
        rows += [lower[k * half:(k + 1) * half], upper[k * half:(k + 1) * half]]
    return rows_of(rows)


def closing(left_ref, kept_ref, mixed_ref, out_ref):
    units, pairs = mixed_ref.shape[0], kept_ref.shape[1] // GATE
    flat = mixed_ref.reshape(units * 4 * 2 * pairs, LANES)
    left = left_ref[...]
    for p in range(pairs // AT_ONCE):
        parts = []
        for q in range(AT_ONCE):
            ap = AT_ONCE * p + q
            pair = [
                rows_of([
                    flat[pl.ds((c * 2 + h) * 2 * pairs + ap * 2 + b, units, stride=8 * pairs), :]
                    for c in range(2) for b in range(2)
                ])
                for h in range(2)
            ]
            parts.append(in_order(*pair))
        y = apply(left, jnp.concatenate(parts, axis=1))
        for q in range(AT_ONCE):
            ap = AT_ONCE * p + q
            for c in range(2):
                pair = weave(
                    kept_ref[c, ap * GATE:(ap + 1) * GATE, :],
                    y[c * GATE:(c + 1) * GATE, q * LANES:(q + 1) * LANES],
                )
                for h in range(2):
                    out_ref[h, pl.ds(ap * 2 * GATE + c, GATE, stride=2), :] = pair[h]


def kernel(narrow, wide, gates_hbm, roster_hbm, x_hbm, kept_hbm, mixed_hbm, last_hbm,
           gates_ref, roster_ref, x_ref, left_ref, plane, mixed, send_n, recv_n, send_w, recv_w,
           load_sem, x_sem, kept_sem, last_sem, mixed_sem, sent_n, came_n, sent_w, came_w):
    me_n, me_w = lax.axis_index("narrow"), lax.axis_index("wide")
    blocks = x_ref.shape[0] // (2 * GATE)
    half = blocks // 2
    chunks = half // PER_CHUNK
    rows_n, rows_w = GATE // narrow, GATE // wide
    split_rows = blocks * GATE
    block_rows = 2 * GATE

    loads = [
        pltpu.make_async_copy(roster_hbm, roster_ref, load_sem.at[0]),
        pltpu.make_async_copy(gates_hbm, gates_ref, load_sem.at[1]),
    ]
    for load in loads:
        load.start()
    piece = half // PIECES

    def x_load(p, h):
        rows = pl.ds(pl.multiple_of((h * half + p * piece) * block_rows, block_rows), piece * block_rows)
        return pltpu.make_async_copy(x_hbm.at[rows], x_ref.at[rows], x_sem.at[p, h])

    for p in range(PIECES):
        for h in range(2):
            x_load(p, h).start()

    barrier = pltpu.get_barrier_semaphore()

    def greet_n(d, _):
        pl.semaphore_signal(barrier, inc=1, device_id={"narrow": lax.rem(me_n + d, narrow)}, device_id_type=MESH)
        return 0

    def greet_w(d, _):
        pl.semaphore_signal(barrier, inc=1, device_id={"wide": lax.rem(me_w + d, wide)}, device_id_type=MESH)
        return 0

    lax.fori_loop(1, narrow, greet_n, 0)
    lax.fori_loop(1, wide, greet_w, 0)

    def bank(k):
        return block_of(gates_ref[roster_ref[k]])

    loads[0].wait()
    loads[1].wait()
    for i in range(2):
        left_ref[i] = left_of(bank(i))

    def keep(split, ap, y):
        for c in range(2):
            start = pl.multiple_of(split * split_rows + c * half * GATE + ap * GATE, GATE)
            plane[pl.ds(start, GATE), :] = y[c * GATE:(c + 1) * GATE]

    def first(split):
        def step(i, _):
            parts = []
            for q in range(AT_ONCE):
                pair = [
                    rows_of([x_ref[pl.ds(a * block_rows + c, GATE, stride=2), :] for c in range(2)])
                    for a in (AT_ONCE * i + q, AT_ONCE * i + q + half)
                ]
                parts.append(weave(*pair)[split])
            y = apply(left_ref[0], jnp.concatenate(parts, axis=1))
            for q in range(AT_ONCE):
                keep(split, AT_ONCE * i + q, y[:, q * LANES:(q + 1) * LANES])
            return 0

        def steps(p, _):
            if split == 0:
                for h in range(2):
                    x_load(p, h).wait()
            lax.fori_loop(p * (piece // AT_ONCE), (p + 1) * (piece // AT_ONCE), step, 0)
            return 0

        lax.fori_loop(0, PIECES, steps, 0)

    def second(phase, ch):
        rnd, split = phase // 2, phase % 2
        parts = []
        for q in range(PER_CHUNK):
            unit = ch * PER_CHUNK + q
            rows = []
            for c in range(2):
                base = split * split_rows + c * half * GATE + unit
                rows += weave(
                    plane[pl.ds(base, blocks, stride=blocks), :],
                    plane[pl.ds(base + half, blocks, stride=blocks), :],
                )
            parts.append(rows_of(rows))
        y = apply(left_ref[4 * rnd + 1], jnp.concatenate(parts, axis=1))
        for q in range(PER_CHUNK):
            for c in range(2):
                for n in range(narrow):
                    at = (q * 2 + c) * rows_n
                    send_n[phase, ch, n, at:at + rows_n, :] = y[
                        c * GATE + n * rows_n:c * GATE + (n + 1) * rows_n,
                        q * LANES:(q + 1) * LANES,
                    ]
        back = lax.rem(me_w, 2) * lax.rem(ch, 2)
        for d in range(1, narrow):
            to = lax.rem(me_n + back * (narrow - 2 * d) + d, narrow)
            pltpu.make_async_remote_copy(
                src_ref=send_n.at[phase, ch, to],
                dst_ref=recv_n.at[phase, ch, me_n],
                send_sem=sent_n.at[phase, ch],
                recv_sem=came_n.at[phase, ch],
                device_id={"narrow": to},
                device_id_type=MESH,
            ).start()
        recv_n[phase, ch, me_n] = send_n[phase, ch, me_n]

    def third(phase, ch):
        rnd = phase // 2
        pltpu.make_async_copy(
            send_n.at[phase, ch, pl.ds(0, narrow - 1)],
            recv_n.at[phase, ch, pl.ds(0, narrow - 1)],
            came_n.at[phase, ch],
        ).wait()
        x = jnp.concatenate(
            [
                rows_of([
                    recv_n[phase, ch, n, pl.ds((q * 2 + c) * rows_n, rows_n), :]
                    for c in range(2) for n in range(narrow)
                ])
                for q in range(PER_CHUNK)
            ],
            axis=1,
        )
        y = apply(left_ref[4 * rnd + 2], x)
        for q in range(PER_CHUNK):
            for c in range(2):
                for w in range(wide):
                    at = (q * 2 + c) * rows_w
                    send_w[phase, ch, w, at:at + rows_w, :] = y[
                        c * GATE + w * rows_w:c * GATE + (w + 1) * rows_w,
                        q * LANES:(q + 1) * LANES,
                    ]

        def push(d, _):
            to = lax.rem(me_w + lax.rem(me_w, 2) * (wide - 2 * d) + d, wide)
            pltpu.make_async_remote_copy(
                src_ref=send_w.at[phase, ch, to],
                dst_ref=recv_w.at[phase, ch, me_w],
                send_sem=sent_w.at[phase, ch],
                recv_sem=came_w.at[phase, ch],
                device_id={"wide": to},
                device_id_type=MESH,
            ).start()
            return 0

        lax.fori_loop(1, wide, push, 0, unroll=wide <= 8)
        recv_w[phase, ch, me_w] = send_w[phase, ch, me_w]

    def fourth(phase, ch):
        rnd, split = phase // 2, phase % 2
        pltpu.make_async_copy(
            send_w.at[phase, ch, pl.ds(0, wide - 1)],
            recv_w.at[phase, ch, pl.ds(0, wide - 1)],
            came_w.at[phase, ch],
        ).wait()
        x = jnp.concatenate(
            [
                rows_of([
                    recv_w[phase, ch, w, pl.ds((q * 2 + c) * rows_w, rows_w), :]
                    for c in range(2) for w in range(wide)
                ])
                for q in range(PER_CHUNK)
            ],
            axis=1,
        )
        y = apply(left_ref[4 * rnd + 3], x)
        for q in range(PER_CHUNK):
            unit = ch * PER_CHUNK + q
            start = pl.multiple_of(split * split_rows + unit * block_rows, block_rows)
            mixed[pl.ds(start, block_rows), :] = y[:, q * LANES:(q + 1) * LANES]

    def fifth(phase):
        rnd, split = phase // 2, phase % 2

        def step(i, _):
            parts = []
            for q in range(AT_ONCE):
                pair = [
                    rows_of([
                        mixed[pl.ds(split * split_rows + c * GATE + a * 2 + b, half, stride=block_rows), :]
                        for c in range(2) for b in range(2)
                    ])
                    for a in (AT_ONCE * i + q, AT_ONCE * i + q + half)
                ]
                parts.append(in_order(*pair))
            y = apply(left_ref[4 * rnd + 4], jnp.concatenate(parts, axis=1))
            for q in range(AT_ONCE):
                ap = AT_ONCE * i + q
                keep(split, ap, y[:, q * LANES:(q + 1) * LANES])
            return 0

        lax.fori_loop(0, half // AT_ONCE, step, 0)

    def over_chunks(body):
        def step(ch, _):
            body(ch)
            return 0

        lax.fori_loop(0, chunks, step, 0)

    first(0)
    pl.semaphore_wait(barrier, narrow - 1 + wide - 1)
    over_chunks(lambda ch: second(0, ch))
    first(1)
    for rnd in range(ROUNDS):
        for i in range(max(2 - 4 * rnd, 1), 4):
            if 4 * rnd + i > 1:
                left_ref[4 * rnd + i] = left_of(bank(5 * rnd + i))
        last = bank(5 * rnd + 4)
        if rnd < ROUNDS - 1:
            last = jnp.dot(
                bank(5 * rnd + 5), last, precision=lax.Precision.HIGHEST,
                preferred_element_type=jnp.float32,
            )
        left_ref[4 * rnd + 4] = left_of(last)

    last_out = pltpu.make_async_copy(left_ref.at[4 * ROUNDS], last_hbm, last_sem)
    last_out.start()
    kept_out = pltpu.make_async_copy(plane.at[pl.ds(0, split_rows)], kept_hbm, kept_sem)

    def mixed_out(ch):
        rows = PER_CHUNK * block_rows
        start = pl.multiple_of(ch * rows, rows)
        return pltpu.make_async_copy(
            mixed.at[pl.ds(split_rows + start, rows)], mixed_hbm.at[pl.ds(start, rows)], mixed_sem.at[ch]
        )

    def ending(ch):
        fourth(2 * ROUNDS - 1, ch)
        mixed_out(ch).start()

    def settle(phases, ch):
        for phase in phases:
            pltpu.make_async_copy(
                send_n.at[phase, ch, pl.ds(0, narrow - 1)],
                recv_n.at[phase, ch, pl.ds(0, narrow - 1)],
                sent_n.at[phase, ch],
            ).wait()
            pltpu.make_async_copy(
                send_w.at[phase, ch, pl.ds(0, wide - 1)],
                recv_w.at[phase, ch, pl.ds(0, wide - 1)],
                sent_w.at[phase, ch],
            ).wait()

    for phase in range(2 * ROUNDS):
        def exchange(ch, phase=phase):
            third(phase, ch)
            if phase + 1 < 2 * ROUNDS:
                second(phase + 1, ch)

        over_chunks(exchange)
        if phase + 1 < 2 * ROUNDS:
            over_chunks(functools.partial(fourth, phase))
            fifth(phase)
            if phase == 2 * ROUNDS - 2:
                kept_out.start()
                over_chunks(functools.partial(settle, range(2 * ROUNDS - 1)))
        else:
            over_chunks(ending)

    over_chunks(functools.partial(settle, [2 * ROUNDS - 1]))
    last_out.wait()
    kept_out.wait()
    over_chunks(lambda ch: mixed_out(ch).wait())


def on_device(state, gates, roster):
    narrow, wide = lax.axis_size("narrow"), lax.axis_size("wide")
    rows = state.shape[1] // LANES
    chunks = rows // GATE // 2 // PER_CHUNK
    phases = 2 * ROUNDS
    x = state.reshape(2, rows, LANES).transpose(1, 0, 2).reshape(2 * rows, LANES)
    f32 = jnp.float32
    trade_n = pltpu.VMEM((phases, chunks, narrow, PER_CHUNK * 2 * GATE // narrow, LANES), f32)
    trade_w = pltpu.VMEM((phases, chunks, wide, PER_CHUNK * 2 * GATE // wide, LANES), f32)
    dma = pltpu.SemaphoreType.DMA((phases, chunks))
    hbm = pl.BlockSpec(memory_space=pltpu.HBM)
    whole = pltpu.VMEM((2 * rows, LANES), f32)
    half_state = jax.ShapeDtypeStruct((rows, LANES), f32)
    factor = jax.ShapeDtypeStruct((4 * GATE, 4 * GATE), jnp.bfloat16)
    kept, mixed, last = pl.pallas_call(
        functools.partial(kernel, narrow, wide),
        out_shape=[half_state, half_state, factor],
        in_specs=[hbm, hbm, hbm],
        out_specs=[hbm, hbm, hbm],
        scratch_shapes=[
            pltpu.VMEM(gates.shape, f32),
            pltpu.SMEM(roster.shape, jnp.int32),
            whole,
            pltpu.VMEM((4 * ROUNDS + 1, 4 * GATE, 4 * GATE), jnp.bfloat16),
            whole, whole,
            trade_n, trade_n, trade_w, trade_w,
            pltpu.SemaphoreType.DMA((2,)),
            pltpu.SemaphoreType.DMA((PIECES, 2)),
            pltpu.SemaphoreType.DMA, pltpu.SemaphoreType.DMA,
            pltpu.SemaphoreType.DMA((chunks,)),
            dma, dma, dma, dma,
        ],
        compiler_params=pltpu.CompilerParams(
            collective_id=0, has_side_effects=True, vmem_limit_bytes=64 * 1024 * 1024
        ),
    )(gates, roster, x)

    half = rows // GATE // 2
    pairs = half // STEPS
    out = pl.pallas_call(
        closing,
        grid=(STEPS,),
        out_shape=jax.ShapeDtypeStruct((2, rows, LANES), f32),
        in_specs=[
            pl.BlockSpec((4 * GATE, 4 * GATE), lambda i: (0, 0)),
            pl.BlockSpec((2, pairs * GATE, LANES), lambda i: (0, i, 0)),
            pl.BlockSpec((half, 2, 2, 2 * pairs, LANES), lambda i: (0, 0, 0, i, 0)),
        ],
        out_specs=pl.BlockSpec((2, pairs * 2 * GATE, LANES), lambda i: (0, i, 0)),
        compiler_params=pltpu.CompilerParams(vmem_limit_bytes=64 * 1024 * 1024),
    )(last, kept.reshape(2, half * GATE, LANES), mixed.reshape(half, 2, 2, GATE // 2, LANES))
    return out.reshape(rows, 2, LANES).transpose(1, 0, 2).reshape(2, rows * LANES)


def solution(mesh):
    in_specs = (P(None, ("wide", "narrow")), P(), P())
    out_specs = P(None, ("wide", "narrow"))
    return jax.shard_map(
        on_device, mesh=mesh, in_specs=in_specs, out_specs=out_specs, check_vma=False
    )
```
